512 devices in a mesh: replica: 32 (over z_hi, y, core), fsdp: 16 (over x, z_lo).
Axes of the slice: x: 4, y: 8, z: 8 (z_hi: 2, z_lo: 4; z = z_hi * 4 + z_lo), core: 2. Of those that a mesh axis runs over, the one named last changes fastest.
Arguments:
- hidden: bfloat16 [32, 2, 1024, 8192], P('replica', None, 'fsdp'), may hold values from -6 to 6
- targets: bfloat16 [32, 2, 1024, 512], P('replica', None, 'fsdp'), may hold values from -16 to 16
- doc_ids: int32 [32, 2, 1024], P('replica', None, 'fsdp'), may hold values from 0 to 7, never falling along the last dimension, each value on 1 to 256 neighbouring positions
- weights: bfloat16 [32, 8192, 512], P('replica', 'fsdp'), may hold values from -5 to 5
- adam_m: bfloat16 [32, 8192, 512], P('replica', 'fsdp'), may hold values from -6.67572e-06 to 6.67572e-06
- adam_v: bfloat16 [32, 8192, 512], P('replica', 'fsdp'), may hold values from 9.05942e-14 to 9.094947e-12
- anchor: bfloat16 [8192, 128], P('fsdp'), may hold values from -5 to 5
- momentum: bfloat16 [8192, 128], P('fsdp'), may hold values from -5 to 5
- fragment: int32 [1], replicated, may hold values from 0 to 3
Outputs:
- new_weights: float32 [32, 8192, 512], P('replica', 'fsdp')
- losses: float32 [32, 2], P('replica')
The draws below stay inside these ranges and needn't reach their ends.
Inputs may be any that keep to these rules, and one draw needn't show every extreme that they name: `doc_ids`: in each row (replica, step) the document numbers never fall, every number 0 to 7 occurs, each document has 1 to 256 tokens and one has exactly 256.
All inputs are finite; a program needn't handle non-finite values.
Results may differ from the reference program's by a relative error of at most 0.0003.
Values may be sent and summed in bfloat16 or wider, within the bound.
No kernel may reach another device: no remote copies, remote signals or barrier semaphores. Data moves between devices by JAX's collectives and lax.ppermute only.
A program may use at most 64 MiB of HBM per device.

```python
import math
import jax
import jax.numpy as jnp
import numpy as np
from jax import lax

D = 8192
WV = 512
FRAGS = 4
FW = 128
STEPS = 2
DOCS = 8
TOKENS = 1024
DOC_MOST = 256
N_REPLICA = 32


def draw_targets(key, part):
    key = jax.random.fold_in(key, 11)
    first_key, second_key = jax.random.split(key, 2)
    shape = (N_REPLICA, STEPS, TOKENS, WV)
    base = jax.random.truncated_normal(first_key, -4.0, 4.0, shape, jnp.float32)
    spread = jnp.exp(jax.random.uniform(second_key, (N_REPLICA, STEPS, TOKENS, 1), jnp.float32, math.log(0.3), math.log(3.0)))
    return (base * spread).astype(jnp.bfloat16)


def steps_of(own_key, dims, cuts, smallest, high):
    gain = 1.0
    for axis_at, shards_of in cuts:
        draws = jax.random.uniform(jax.random.fold_in(jax.random.fold_in(own_key, 6), axis_at), (shards_of,), jnp.float32, smallest / len(cuts), high / len(cuts))
        gain = gain * jnp.repeat(jnp.exp(draws), dims[axis_at] // shards_of).reshape((-1,) + (1,) * (len(dims) - 1 - axis_at))
    return gain


def split_up(count, total, most, slope):
    portions = [(1 << 20) // math.isqrt(rank ** slope) + 1 for rank in range(2, count + 1)]
    rest, given = total - most - (count - 1), [1] * (count - 1)
    while rest > 0:
        candidates = [i for i in range(count - 1) if given[i] < most]
        whole, budget = sum([portions[i] for i in candidates]), rest
        for i in candidates:
            addition = min(most - given[i], max(1, budget * portions[i] // whole), rest)
            given[i] = given[i] + addition
            rest = rest - addition
    return np.array([most] + given)


def uneven(own_key, count, total, limit, lean):
    if count == 2:
        one = jax.random.randint(own_key, (), max(1, total - limit), min(limit, total - 1) + 1)
        return jnp.stack([one, total - one])
    sizes = jnp.asarray(split_up(count, total, limit, lean), jnp.int32)
    pairs = (count - 1) // 2
    source_of, taker = sizes[1:1 + 2 * pairs:2], sizes[2:2 + 2 * pairs:2]
    room = jnp.minimum(source_of - 1, limit - taker)
    moved = jax.random.randint(jax.random.fold_in(own_key, 1), (pairs,), 0, 1 << 20) % (room + 1)
    sizes = sizes.at[1:1 + 2 * pairs:2].set(source_of - moved).at[2:2 + 2 * pairs:2].set(taker + moved)
    return sizes[jax.random.permutation(jax.random.fold_in(own_key, 2), count)]


def noise(key, extent, scale, most, cuts=(), held_as=jnp.bfloat16):
    values = scale * jax.random.normal(key, extent, jnp.float32)
    if cuts:
        values = values * steps_of(key, extent, cuts, -0.22, 0.18)
    return jnp.clip(values, -most, most).astype(held_as)


def setup_inputs(seed: int = 0) -> dict:
    key_list = jax.random.split(jax.random.key(seed), 10)
    return {
        "hidden": noise(key_list[0], (N_REPLICA, STEPS, TOKENS, D), 1.0, 6.0, ((0, 32), (2, 16))),
        "targets": draw_targets(jax.random.fold_in(key_list[9], 71), 0),
        "doc_ids": jax.vmap(lambda own: jnp.searchsorted(jnp.cumsum(uneven(own, DOCS, TOKENS, DOC_MOST, 1)), jnp.arange(TOKENS), side="right"))(jax.random.split(key_list[2], N_REPLICA * STEPS)).reshape((N_REPLICA, STEPS, TOKENS)).astype(jnp.int32),
        "weights": noise(key_list[3], (N_REPLICA, D, WV), 1.0, 5.0, ((0, 32), (1, 16))),
        "adam_m": noise(key_list[4], (N_REPLICA, D, WV), (0.7 / (WV * (D * TOKENS) ** 0.5)), 6.67572021484375e-06, ((0, 32), (1, 16))),
        "adam_v": jnp.clip(jnp.exp(math.log(9.094947017729282e-12) - 4.609084 * jax.random.uniform(key_list[5], (N_REPLICA, D, WV), jnp.float32) ** steps_of(key_list[5], (N_REPLICA, D, WV), ((0, 32), (1, 16)), -0.2, 0.2)), 9.059419880941277e-14, 9.094947017729282e-12).astype(jnp.bfloat16),
        "anchor": noise(key_list[6], (D, FW), 1.0, 5.0, ((0, 16),)),
        "momentum": noise(key_list[7], (D, FW), 1.0, 5.0, ((0, 16),)),
        "fragment": jax.random.randint(key_list[8], (1,), 0, FRAGS).astype(jnp.int32),
    }


NORM_EPS = 1e-05
ADAM_EPS = 1e-08
INNER_RATE = 0.1
DECAY_RATE = 0.1
BETA_FIRST = 0.9
BETA_SECOND = 0.95
OUTER_RATE = 0.7
NESTEROV = 0.9
MIXING = 0.5

def normalize(block):
    wide = block.astype(jnp.float32)
    power = lax.optimization_barrier(jnp.mean(wide * wide, axis=-1, keepdims=True))
    return (wide * lax.rsqrt(power + NORM_EPS)).astype(jnp.bfloat16)

def token_weights(labels):
    onehot = (labels[:, None] == jnp.arange(DOCS, dtype=jnp.int32)[None, :]).astype(jnp.float32)
    counts = lax.optimization_barrier(jnp.sum(onehot, axis=0))
    inverse = 1.0 / (DOCS * counts)
    return jnp.dot(onehot, inverse, precision=lax.Precision.HIGHEST)

def adam_update(master, first, second, gradient):
    first = BETA_FIRST * first + (1.0 - BETA_FIRST) * gradient
    second = BETA_SECOND * second + (1.0 - BETA_SECOND) * gradient * gradient
    master = master - INNER_RATE * (first / (jnp.sqrt(second) + ADAM_EPS) + DECAY_RATE * master)
    return (master, first, second)

def reference(hidden, targets, doc_ids, weights, adam_m, adam_v, anchor, momentum, fragment):
    zero = jnp.zeros((), jnp.int32)
    start = (fragment[0] * FW).astype(jnp.int32)
    local = lax.dynamic_slice(weights, (zero, zero, start), (N_REPLICA, D, FW))
    delta = anchor.astype(jnp.float32)[None] - local.astype(jnp.float32)
    mean_delta = lax.optimization_barrier(jnp.sum(delta, axis=0)) / N_REPLICA
    new_momentum = NESTEROV * momentum.astype(jnp.float32) + mean_delta
    global_fragment = anchor.astype(jnp.float32) - OUTER_RATE * (mean_delta + NESTEROV * new_momentum)
    scale = D ** (-0.5)

    def replica(packed):
        hidden_rows, target_rows, label_rows, weight_rows, first_rows, second_rows = packed
        master = weight_rows.astype(jnp.float32)
        first = first_rows.astype(jnp.float32)
        second = second_rows.astype(jnp.float32)
        step_losses = []
        for step_index in range(STEPS):
            normed = normalize(hidden_rows[step_index])
            current = master.astype(jnp.bfloat16)
            values = jnp.dot(normed, current, preferred_element_type=jnp.float32) * scale
            error = values - target_rows[step_index].astype(jnp.float32)
            weight_row = token_weights(label_rows[step_index])
            step_losses.append(jnp.sum(weight_row * 0.5 * lax.optimization_barrier(jnp.mean(error * error, axis=-1))))
            error_grad = (weight_row[:, None] * error / WV).astype(jnp.bfloat16)
            gradient = jnp.dot(normed.T, error_grad, preferred_element_type=jnp.float32) * scale
            master, first, second = adam_update(master, first, second, gradient)
        merged = MIXING * lax.dynamic_slice(master, (zero, start), (D, FW)) + (1.0 - MIXING) * global_fragment
        master = lax.dynamic_update_slice(master, merged, (zero, start))
        return (master, jnp.stack(step_losses))
    new_weights, losses = lax.map(replica, (hidden, targets, doc_ids, weights, adam_m, adam_v))
    return (new_weights, losses)
```

```python
import jax
import jax.numpy as jnp
from jax import lax
from jax.sharding import Mesh, PartitionSpec as P

DOCS = 8


NORM_EPS = 1e-05
ADAM_EPS = 1e-08
INNER_RATE = 0.1
DECAY_RATE = 0.1
BETA_FIRST = 0.9
BETA_SECOND = 0.95
OUTER_RATE = 0.7
NESTEROV = 0.9
MIXING = 0.5

REPLICA = ("zh", "y", "c")
FSDP = ("x", "zl")
EXTRA = 16


def normalize(block):
    wide = block.astype(jnp.float32)
    power = jnp.mean(wide * wide, axis=-1, keepdims=True)
    return (wide * lax.rsqrt(power + NORM_EPS)).astype(jnp.bfloat16)


def adam_update(master, first, second, gradient):
    first = BETA_FIRST * first + (1.0 - BETA_FIRST) * gradient
    second = BETA_SECOND * second + (1.0 - BETA_SECOND) * gradient * gradient
    master = master - INNER_RATE * (first / (jnp.sqrt(second) + ADAM_EPS) + DECAY_RATE * master)
    return (master, first, second)


def exchange(blocks, axes):
    return lax.all_to_all(blocks, axes, split_axis=0, concat_axis=0, tiled=False)


def split_up(value):
    high = value.astype(jnp.bfloat16)
    rest = value - high.astype(jnp.float32)
    middle = rest.astype(jnp.bfloat16)
    low = (rest - middle.astype(jnp.float32)).astype(jnp.bfloat16)
    return high, middle, low


def body(hidden, targets, doc_ids, weights, adam_m, adam_v, anchor, momentum, fragment):
    steps_total, rows, model_width = hidden.shape[1:]
    shard_rows, value_width = weights.shape[1:]
    frag_width = anchor.shape[1]
    nx, nz = lax.axis_size("x"), lax.axis_size("zl")
    shards = nx * nz
    scale = model_width ** (-0.5)
    zero = jnp.zeros((), jnp.int32)
    start = fragment[0] * frag_width
    replicas = lax.axis_size(REPLICA)

    doc_range = jnp.arange(DOCS, dtype=jnp.int32)
    onehot = (doc_ids[0][..., None] == doc_range).astype(jnp.float32)
    local_counts = jnp.sum(onehot, axis=1).reshape(1, 1, -1)
    count_rows = jnp.pad(
        local_counts.astype(jnp.bfloat16),
        ((0, 0), (0, EXTRA - 1), (0, value_width - steps_total * DOCS)),
    )

    columns = []
    for step_index in range(steps_total):
        normed = normalize(hidden[0, step_index])
        blocks = normed.reshape(rows, shards, shard_rows).transpose(1, 0, 2)
        columns.append(exchange(blocks, FSDP).reshape(shards * rows, shard_rows))

    local = lax.dynamic_slice(weights[0], (zero, start), (shard_rows, frag_width))
    pieces = exchange(local.reshape(replicas, shard_rows // replicas, frag_width), REPLICA)
    mean_piece = jnp.sum(pieces.astype(jnp.float32), axis=0) / replicas
    mean_weights = exchange(
        jnp.broadcast_to(mean_piece[None], (replicas,) + mean_piece.shape), REPLICA
    ).reshape(shard_rows, frag_width)
    anchor_rows = anchor.astype(jnp.float32)
    mean_delta = anchor_rows - mean_weights
    new_moment = NESTEROV * momentum.astype(jnp.float32) + mean_delta
    global_fragment = anchor_rows - OUTER_RATE * (mean_delta + NESTEROV * new_moment)

    master = weights[0].astype(jnp.float32)
    first = adam_m[0].astype(jnp.float32)
    second = adam_v[0].astype(jnp.float32)
    losses = []
    inverse = None
    for step_index in range(steps_total):
        current = master.astype(jnp.bfloat16)
        partial = jnp.dot(columns[step_index], current, preferred_element_type=jnp.float32)
        partial = partial.astype(jnp.bfloat16).reshape(nx, nz, rows, value_width)
        if step_index == 0:
            extra = jnp.broadcast_to(count_rows[None], (nx, nz, EXTRA, value_width))
            partial = jnp.concatenate([partial, extra], axis=2)
        block = partial.shape[2]
        partial = exchange(partial.reshape(nx, nz * block, value_width), "x")
        partial = jnp.sum(partial.astype(jnp.float32), axis=0).astype(jnp.bfloat16)
        partial = exchange(partial.reshape(nz, block, value_width), "zl")
        total = jnp.sum(partial.astype(jnp.float32), axis=0)
        if step_index == 0:
            counts = total[rows, : steps_total * DOCS].reshape(steps_total, DOCS)
            inverse = 1.0 / (DOCS * counts)
        values = total[:rows] * scale
        weight_row = jnp.sum(onehot[step_index] * inverse[step_index][None], axis=1)
        error = values - targets[0, step_index].astype(jnp.float32)
        loss = jnp.sum(weight_row * 0.5 * jnp.mean(error * error, axis=-1))
        error_grad = (weight_row[:, None] * error / value_width).astype(jnp.bfloat16)
        terms = jnp.stack(split_up(loss)).reshape(1, 3)
        loss_rows = jnp.pad(terms, ((0, EXTRA - 1), (0, value_width - 3)))
        sent = jnp.concatenate([error_grad, loss_rows], axis=0)
        got = exchange(jnp.broadcast_to(sent[None], (nz,) + sent.shape), "zl")
        got = exchange(jnp.broadcast_to(got[None], (nx,) + got.shape), "x")
        got = got.reshape(shards, rows + EXTRA, value_width)
        losses.append(jnp.sum(got[:, rows, :3].astype(jnp.float32)))
        everyone = got[:, :rows].reshape(shards * rows, value_width)
        gradient = (
            lax.dot_general(
                columns[step_index],
                everyone,
                (((0,), (0,)), ((), ())),
                preferred_element_type=jnp.float32,
            )
            * scale
        )
        master, first, second = adam_update(master, first, second, gradient)
    merged = (
        MIXING * lax.dynamic_slice(master, (zero, start), (shard_rows, frag_width))
        + (1.0 - MIXING) * global_fragment
    )
    master = lax.dynamic_update_slice(master, merged, (zero, start))
    return (master[None], jnp.stack(losses)[None])


def solution(mesh):
    fine = Mesh(mesh.devices.reshape(2, 8, 2, 4, 4), REPLICA + FSDP)
    placed = (
        P(REPLICA, None, FSDP, None),
        P(REPLICA, None, FSDP, None),
        P(REPLICA, None, FSDP),
        P(REPLICA, FSDP, None),
        P(REPLICA, FSDP, None),
        P(REPLICA, FSDP, None),
        P(FSDP, None),
        P(FSDP, None),
        P(),
    )
    return jax.shard_map(
        body,
        mesh=fine,
        in_specs=placed,
        out_specs=(P(REPLICA, FSDP, None), P(REPLICA, None)),
        check_vma=False,
    )
```

```python
import functools

import jax
import jax.numpy as jnp
from jax import lax
from jax.experimental import pallas as pl
from jax.experimental.pallas import tpu as pltpu
from jax.sharding import Mesh, PartitionSpec as P

DOCS = 8


NORM_EPS = 1e-05
ADAM_EPS = 1e-08
INNER_RATE = 0.1
DECAY_RATE = 0.1
BETA_FIRST = 0.9
BETA_SECOND = 0.95
OUTER_RATE = 0.7
NESTEROV = 0.9
MIXING = 0.5

REPLICA = ("zh", "y", "c")
FSDP = ("x", "zf", "zn")
ORDER = ("x", "zn", "zf")
GROUP = ("x", "zn")
EXTRA = 16
CHUNK = 16
VMEM = 48 * 1024 * 1024

bf16, f32 = jnp.bfloat16, jnp.float32


def adam_update(master, first, second, gradient):
    first = BETA_FIRST * first + (1.0 - BETA_FIRST) * gradient
    second = BETA_SECOND * second + (1.0 - BETA_SECOND) * gradient * gradient
    master = master - INNER_RATE * (first / (jnp.sqrt(second) + ADAM_EPS) + DECAY_RATE * master)
    return (master, first, second)


def exchange(blocks, axes):
    return lax.all_to_all(blocks, axes, split_axis=0, concat_axis=0, tiled=False)


def swap(block, axis, bit=1):
    size = lax.axis_size(axis)
    return lax.ppermute(block, axis, [(i, i ^ bit) for i in range(size)])


def tie(*values):
    return lax.optimization_barrier(values)


def normalize_kernel(width, hidden_ref, out_ref):
    wide = hidden_ref[0, 0].astype(f32)
    power = jnp.mean(wide * wide, axis=-1, keepdims=True)
    normed = (wide * lax.rsqrt(power + NORM_EPS)).astype(bf16)
    for at in range(out_ref.shape[0]):
        x, zn, zf = at // 4, (at // 2) % 2, at % 2
        owner = x * 4 + zf * 2 + zn
        out_ref[at] = normed[:, owner * width : (owner + 1) * width]


def normalize(hidden, step, shards):
    rows, model_width = hidden.shape[2:]
    width = model_width // shards
    return pl.pallas_call(
        functools.partial(normalize_kernel, width),
        grid=(rows // CHUNK,),
        in_specs=[pl.BlockSpec((1, 1, CHUNK, model_width), lambda i: (0, step, i, 0))],
        out_specs=pl.BlockSpec((shards, CHUNK, width), lambda i: (0, i, 0)),
        out_shape=jax.ShapeDtypeStruct((shards, rows, width), bf16),
        compiler_params=pltpu.CompilerParams(vmem_limit_bytes=VMEM),
        cost_estimate=pl.CostEstimate(
            flops=4 * rows * model_width, bytes_accessed=4 * rows * model_width, transcendentals=rows
        ),
        name="normalize",
    )(hidden)


def error_kernel(scale, with_counts, own_ref, got_ref, target_ref, hot_ref, *rest):
    if with_counts:
        out_ref, inverse_ref = rest
    else:
        inverse_in_ref, out_ref = rest
    tokens, columns = target_ref.shape
    total = own_ref[:tokens] + got_ref[:tokens].astype(f32)
    if with_counts:
        counts = (own_ref[tokens:] + got_ref[tokens:].astype(f32))[:1, :128]
        inverse = jnp.where(counts > 0.0, 1.0 / (DOCS * jnp.maximum(counts, 1.0)), 0.0)
        inverse_ref[...] = jnp.broadcast_to(inverse, inverse_ref.shape)
    else:
        inverse = inverse_in_ref[:1]
    weight = jnp.sum(hot_ref[...] * inverse, axis=-1, keepdims=True)
    error = total * scale - target_ref[...].astype(f32)
    grad = (weight * error / columns).astype(bf16)
    each = jnp.sum(error * error, axis=-1, keepdims=True) / columns
    loss = jnp.sum(weight * 0.5 * each, axis=0, keepdims=True)
    high = loss.astype(bf16).astype(f32)
    middle = (loss - high).astype(bf16).astype(f32)
    low = loss - high - middle
    lane = lax.broadcasted_iota(jnp.int32, (EXTRA, columns), 1)
    row = jnp.where(lane == 0, high, jnp.where(lane == 1, middle, jnp.where(lane == 2, low, 0.0)))
    row = row.astype(bf16)
    for at in range(out_ref.shape[0]):
        out_ref[at, :tokens] = grad
        out_ref[at, tokens:] = row


def errors(own, got, target, hot, inverse, copies, scale):
    tokens, columns = target.shape
    sent = jax.ShapeDtypeStruct((copies, tokens + EXTRA, columns), bf16)
    kept = jax.ShapeDtypeStruct((8, 128), f32)
    with_counts = inverse is None
    return pl.pallas_call(
        functools.partial(error_kernel, scale, with_counts),
        out_shape=(sent, kept) if with_counts else sent,
        compiler_params=pltpu.CompilerParams(vmem_limit_bytes=VMEM),
        cost_estimate=pl.CostEstimate(
            flops=8 * tokens * columns, bytes_accessed=30 * tokens * columns, transcendentals=0
        ),
        name="errors",
    )(own, got, target, hot, *(() if with_counts else (inverse,)))


def body(hidden, targets, doc_ids, weights, adam_m, adam_v, anchor, momentum, fragment):
    steps_total, rows, model_width = hidden.shape[1:]
    shard_rows, value_width = weights.shape[1:]
    frag_width = anchor.shape[1]
    nx, nn, nf = (lax.axis_size(a) for a in ORDER)
    shards, groups = nx * nn * nf, nx * nn
    x_at, n_at, f_at = (lax.axis_index(a) for a in ORDER)
    scale = model_width ** (-0.5)
    zero = jnp.zeros((), jnp.int32)
    start = fragment[0] * frag_width
    replicas = lax.axis_size(REPLICA)
    tokens = nf * rows

    def pick(array, at, axis):
        return lax.dynamic_index_in_dim(array, at, axis, keepdims=False)

    blocks = normalize(hidden, 0, shards)
    blocks, hidden, weights, targets, doc_ids = tie(blocks, hidden, weights, targets, doc_ids)
    columns = exchange(blocks, ORDER).reshape(shards * rows, shard_rows)

    blocks = normalize(hidden, 1, shards).reshape(nx, nn, nf, rows, shard_rows)
    over_x = [pick(blocks, x_at, 0)]
    for bit in range(1, nx):
        over_x.append(swap(pick(blocks, x_at ^ bit, 0), "x", bit))
    over_x = jnp.stack(over_x)
    over_x = jnp.stack([pick(over_x, x_at ^ at, 0) for at in range(nx)])
    kept = pick(over_x, n_at, 1)
    given = swap(pick(over_x, n_at ^ 1, 1), "zn")
    near = jnp.stack(
        [jnp.where(n_at == 0, kept, given), jnp.where(n_at == 0, given, kept)], axis=1
    )
    far_kept = pick(near, f_at, 2)
    far_sent = pick(near, f_at ^ 1, 2)

    id_rows = jnp.pad(
        doc_ids[0].astype(bf16)[:, None, :],
        ((0, 0), (0, EXTRA - 1), (0, value_width - rows)),
    )
    own_rows = jnp.concatenate([targets[0], id_rows], axis=1)
    far_rows = swap(own_rows, "zf")
    pair = jnp.stack(
        [jnp.where(f_at == 0, own_rows, far_rows), jnp.where(f_at == 0, far_rows, own_rows)], axis=1
    )
    pair_targets = pair[:, :, :rows].reshape(steps_total, tokens, value_width)
    pair_ids = pair[:, :, rows, :rows].reshape(steps_total, tokens, 1).astype(jnp.int32)
    step_shift = DOCS * jnp.arange(steps_total, dtype=jnp.int32)[:, None, None]
    hot = (pair_ids + step_shift == jnp.arange(128, dtype=jnp.int32)).astype(f32)

    local = lax.dynamic_slice(weights[0], (zero, start), (shard_rows, frag_width))
    summed = local.astype(f32) + swap(local, "zh").astype(f32)
    summed = summed + swap(summed, "c")

    doc_range = jnp.arange(DOCS, dtype=jnp.int32)
    own_hot = (doc_ids[0][..., None] == doc_range).astype(f32)
    count_rows = jnp.pad(
        jnp.sum(own_hot, axis=1).reshape(1, 1, -1).astype(bf16),
        ((0, 0), (0, EXTRA - 1), (0, value_width - steps_total * DOCS)),
    )

    columns, far_kept, far_sent, pair_targets, hot, summed = tie(
        columns, far_kept, far_sent, pair_targets, hot, summed
    )
    summed = lax.psum(summed, "y")

    master = weights[0].astype(f32)
    first = adam_m[0].astype(f32)
    second = adam_v[0].astype(f32)
    losses = []
    inverse = None
    for step in range(steps_total):
        current = master.astype(bf16)
        partial = jnp.dot(columns, current, preferred_element_type=f32)
        partial = partial.astype(bf16).reshape(groups, tokens, value_width)
        if step == 0:
            extra = jnp.broadcast_to(count_rows, (groups, EXTRA, value_width))
            partial = jnp.concatenate([partial, extra], axis=1)
        partial = exchange(partial, GROUP)
        if step == 0:
            far_a = swap(far_sent[: nx // 2], "zf")
            partial, far_a = tie(partial, far_a)
        own = jnp.sum(partial.astype(f32), axis=0)
        got = swap(own.astype(bf16), "zf")
        sent = errors(own, got, pair_targets[step], hot[step], inverse, groups, scale)
        if step == 0:
            sent, inverse = sent
        if step == 0:
            sent, far_sent = tie(sent, far_sent)
        got = exchange(sent, GROUP)
        if step == 0:
            far_b = swap(far_sent[nx // 2 :], "zf")
            far_given = jnp.concatenate([far_a, far_b], axis=0)
            later = jnp.stack(
                [
                    jnp.where(f_at == 0, far_kept, far_given),
                    jnp.where(f_at == 0, far_given, far_kept),
                ],
                axis=2,
            ).reshape(shards * rows, shard_rows)
            got, later = tie(got, later)
        losses.append(jnp.sum(got[:, tokens, :3].astype(f32)))
        everyone = got[:, :tokens].reshape(shards * rows, value_width)
        gradient = (
            lax.dot_general(
                columns, everyone, (((0,), (0,)), ((), ())), preferred_element_type=f32
            )
            * scale
        )
        master, first, second = adam_update(master, first, second, gradient)
        columns = later

    anchor_rows = anchor.astype(f32)
    mean_delta = anchor_rows - summed / replicas
    new_moment = NESTEROV * momentum.astype(f32) + mean_delta
    global_fragment = anchor_rows - OUTER_RATE * (mean_delta + NESTEROV * new_moment)
    merged = (
        MIXING * lax.dynamic_slice(master, (zero, start), (shard_rows, frag_width))
        + (1.0 - MIXING) * global_fragment
    )
    master = lax.dynamic_update_slice(master, merged, (zero, start))
    return (master[None], jnp.stack(losses)[None])


def solution(mesh):
    fine = Mesh(mesh.devices.reshape(2, 8, 2, 4, 2, 2), REPLICA + FSDP)
    placed = (
        P(REPLICA, None, FSDP, None),
        P(REPLICA, None, FSDP, None),
        P(REPLICA, None, FSDP),
        P(REPLICA, FSDP, None),
        P(REPLICA, FSDP, None),
        P(REPLICA, FSDP, None),
        P(FSDP, None),
        P(FSDP, None),
        P(),
    )
    return jax.shard_map(
        body,
        mesh=fine,
        in_specs=placed,
        out_specs=(P(REPLICA, FSDP, None), P(REPLICA, None)),
        check_vma=False,
    )
```

```python
import functools

import jax
import jax.numpy as jnp
from jax import lax
from jax.experimental import pallas as pl
from jax.experimental.pallas import tpu as pltpu
from jax.sharding import Mesh, PartitionSpec as P

DOCS = 8


NORM_EPS = 1e-05
ADAM_EPS = 1e-08
INNER_RATE = 0.1
DECAY_RATE = 0.1
BETA_FIRST = 0.9
BETA_SECOND = 0.95
OUTER_RATE = 0.7
NESTEROV = 0.9
MIXING = 0.5

REPLICA = ("zh", "y", "c")
FSDP = ("x", "zf", "zn")
ORDER = ("x", "zn", "zf")
GROUP = ("x", "zn")
EXTRA = 16
CHUNK = 16
VMEM = 48 * 1024 * 1024

bf16, f32 = jnp.bfloat16, jnp.float32


def adam_update(master, first, second, gradient):
    first = BETA_FIRST * first + (1.0 - BETA_FIRST) * gradient
    second = BETA_SECOND * second + (1.0 - BETA_SECOND) * gradient * gradient
    master = master - INNER_RATE * (first / (jnp.sqrt(second) + ADAM_EPS) + DECAY_RATE * master)
    return (master, first, second)


def exchange(blocks, axes):
    return lax.all_to_all(blocks, axes, split_axis=0, concat_axis=0, tiled=False)


def swap(block, axis, bit=1):
    size = lax.axis_size(axis)
    return lax.ppermute(block, axis, [(i, i ^ bit) for i in range(size)])


def tie(*values):
    return lax.optimization_barrier(values)


def normalize_kernel(width, hidden_ref, out_ref):
    wide = hidden_ref[0, 0].astype(f32)
    power = jnp.mean(wide * wide, axis=-1, keepdims=True)
    normed = (wide * lax.rsqrt(power + NORM_EPS)).astype(bf16)
    for at in range(out_ref.shape[0]):
        x, zn, zf = at // 4, (at // 2) % 2, at % 2
        owner = x * 4 + zf * 2 + zn
        out_ref[at, 0] = normed[:, owner * width : (owner + 1) * width]


def normalize(hidden, shards):
    _, steps, rows, model_width = hidden.shape
    width = model_width // shards
    return pl.pallas_call(
        functools.partial(normalize_kernel, width),
        grid=(steps, rows // CHUNK),
        in_specs=[pl.BlockSpec((1, 1, CHUNK, model_width), lambda s, i: (0, s, i, 0))],
        out_specs=pl.BlockSpec((shards, 1, CHUNK, width), lambda s, i: (0, s, i, 0)),
        out_shape=jax.ShapeDtypeStruct((shards, steps, rows, width), bf16),
        compiler_params=pltpu.CompilerParams(vmem_limit_bytes=VMEM),
        cost_estimate=pl.CostEstimate(
            flops=8 * rows * model_width, bytes_accessed=8 * rows * model_width, transcendentals=rows
        ),
        name="normalize",
    )(hidden)


def error_kernel(scale, own_ref, got_ref, target_ref, weight_ref, out_ref):
    tokens, columns = target_ref.shape
    weight = weight_ref[...]
    values = (own_ref[...] + got_ref[...].astype(f32)) * scale
    error = values - target_ref[...].astype(f32)
    grad = (weight * error / columns).astype(bf16)
    each = jnp.sum(error * error, axis=-1, keepdims=True) / columns
    loss = jnp.sum(weight * 0.5 * each, axis=0, keepdims=True)
    high = loss.astype(bf16).astype(f32)
    middle = (loss - high).astype(bf16).astype(f32)
    low = loss - high - middle
    lane = lax.broadcasted_iota(jnp.int32, (EXTRA, columns), 1)
    row = jnp.where(lane == 0, high, jnp.where(lane == 1, middle, jnp.where(lane == 2, low, 0.0)))
    row = row.astype(bf16)
    for at in range(out_ref.shape[0]):
        out_ref[at, :tokens] = grad
        out_ref[at, tokens:] = row


def errors(own, got, target, weight, copies, scale):
    tokens, columns = target.shape
    return pl.pallas_call(
        functools.partial(error_kernel, scale),
        out_shape=jax.ShapeDtypeStruct((copies, tokens + EXTRA, columns), bf16),
        compiler_params=pltpu.CompilerParams(vmem_limit_bytes=VMEM),
        cost_estimate=pl.CostEstimate(
            flops=8 * tokens * columns, bytes_accessed=30 * tokens * columns, transcendentals=0
        ),
        name="errors",
    )(own, got, target, weight)


def body(hidden, targets, doc_ids, weights, adam_m, adam_v, anchor, momentum, fragment):
    steps_total, rows, model_width = hidden.shape[1:]
    shard_rows, value_width = weights.shape[1:]
    frag_width = anchor.shape[1]
    nx, nn, nf = (lax.axis_size(a) for a in ORDER)
    shards, groups = nx * nn * nf, nx * nn
    f_at, c_at = lax.axis_index("zf"), lax.axis_index("c")
    scale = model_width ** (-0.5)
    zero = jnp.zeros((), jnp.int32)
    start = fragment[0] * frag_width
    replicas = lax.axis_size(REPLICA)
    tokens = nf * rows

    def pick(array, at, axis):
        return lax.dynamic_index_in_dim(array, at, axis, keepdims=False)

    blocks = normalize(hidden, shards)
    blocks, weights, targets, doc_ids = tie(blocks, weights, targets, doc_ids)
    columns = exchange(blocks, ORDER)

    id_rows = jnp.pad(
        doc_ids[0].astype(bf16)[:, None, :],
        ((0, 0), (0, EXTRA - 1), (0, value_width - rows)),
    )
    own_rows = jnp.concatenate([targets[0], id_rows], axis=1)
    far_rows = swap(own_rows, "zf")
    pair = jnp.stack(
        [jnp.where(f_at == 0, own_rows, far_rows), jnp.where(f_at == 0, far_rows, own_rows)], axis=1
    )
    pair_targets = pair[:, :, :rows].reshape(steps_total, tokens, value_width)
    pair_ids = pair[:, :, rows, :rows].reshape(steps_total, tokens, 1).astype(jnp.int32)
    doc_range = jnp.arange(DOCS, dtype=jnp.int32)
    counts = jnp.sum((doc_ids[0][..., None] == doc_range).astype(f32), axis=1)
    for axis, bit in (("x", 1), ("x", 2), ("zn", 1), ("zf", 1)):
        counts = counts + swap(counts, axis, bit)
    inverse = 1.0 / (DOCS * counts)
    hot = (pair_ids == doc_range).astype(f32)
    token_weight = jnp.sum(hot * inverse[:, None, :], axis=-1, keepdims=True)

    half = shard_rows // 2
    local = lax.dynamic_slice(weights[0], (zero, start), (shard_rows, frag_width))
    local = local.reshape(2, half, frag_width)
    summed = pick(local, c_at, 0).astype(f32) + swap(pick(local, c_at ^ 1, 0), "c").astype(f32)
    for bit in (1, 2, 4):
        summed = summed + swap(summed, "y", bit)

    columns, pair_targets, token_weight, summed = tie(columns, pair_targets, token_weight, summed)

    master = weights[0].astype(f32)
    first = adam_m[0].astype(f32)
    second = adam_v[0].astype(f32)
    losses = []
    for step in range(steps_total):
        current = master.astype(bf16)
        rows_now = columns[:, step].reshape(shards * rows, shard_rows)
        partial = jnp.dot(rows_now, current, preferred_element_type=f32)
        partial = partial.astype(bf16).reshape(groups, tokens, value_width)
        partial = exchange(partial, GROUP)
        if step == 0:
            summed = summed + swap(summed, "zh")
            partial, summed = tie(partial, summed)
        own = jnp.sum(partial.astype(f32), axis=0)
        got = swap(own.astype(bf16), "zf")
        sent = errors(own, got, pair_targets[step], token_weight[step], groups, scale)
        if step == 0:
            sent, summed = tie(sent, summed)
        got = exchange(sent, GROUP)
        if step == 0:
            other = swap(summed, "c")
            got, summed, other = tie(got, summed, other)
        losses.append(jnp.sum(got[:, tokens, :3].astype(f32)))
        everyone = got[:, :tokens].reshape(shards * rows, value_width)
        gradient = (
            lax.dot_general(
                rows_now, everyone, (((0,), (0,)), ((), ())), preferred_element_type=f32
            )
            * scale
        )
        master, first, second = adam_update(master, first, second, gradient)

    anchor_rows = anchor.astype(f32)
    summed = jnp.concatenate(
        [jnp.where(c_at == 0, summed, other), jnp.where(c_at == 0, other, summed)], axis=0
    )
    mean_delta = anchor_rows - summed / replicas
    new_moment = NESTEROV * momentum.astype(f32) + mean_delta
    global_fragment = anchor_rows - OUTER_RATE * (mean_delta + NESTEROV * new_moment)
    merged = (
        MIXING * lax.dynamic_slice(master, (zero, start), (shard_rows, frag_width))
        + (1.0 - MIXING) * global_fragment
    )
    master = lax.dynamic_update_slice(master, merged, (zero, start))
    return (master[None], jnp.stack(losses)[None])


def solution(mesh):
    fine = Mesh(mesh.devices.reshape(2, 8, 2, 4, 2, 2), REPLICA + FSDP)
    placed = (
        P(REPLICA, None, FSDP, None),
        P(REPLICA, None, FSDP, None),
        P(REPLICA, None, FSDP),
        P(REPLICA, FSDP, None),
        P(REPLICA, FSDP, None),
        P(REPLICA, FSDP, None),
        P(FSDP, None),
        P(FSDP, None),
        P(),
    )
    return jax.shard_map(
        body,
        mesh=fine,
        in_specs=placed,
        out_specs=(P(REPLICA, FSDP, None), P(REPLICA, None)),
        check_vma=False,
    )
```

```python
import functools

import jax
import jax.numpy as jnp
from jax import lax
from jax.experimental import pallas as pl
from jax.experimental.pallas import tpu as pltpu
from jax.sharding import Mesh, PartitionSpec as P

DOCS = 8


NORM_EPS = 1e-05
ADAM_EPS = 1e-08
INNER_RATE = 0.1
DECAY_RATE = 0.1
BETA_FIRST = 0.9
BETA_SECOND = 0.95
OUTER_RATE = 0.7
NESTEROV = 0.9
MIXING = 0.5

REPLICA = ("zh", "y", "c")
FSDP = ("x", "zf", "zn")
ORDER = ("x", "zn", "zf")
GROUP = ("x", "zn")
EXTRA = 16
CHUNK = 32
VMEM = 16 * 1024 * 1024

bf16, f32 = jnp.bfloat16, jnp.float32


def adam_update(master, first, second, gradient):
    first = BETA_FIRST * first + (1.0 - BETA_FIRST) * gradient
    second = BETA_SECOND * second + (1.0 - BETA_SECOND) * gradient * gradient
    master = master - INNER_RATE * (first / (jnp.sqrt(second) + ADAM_EPS) + DECAY_RATE * master)
    return (master, first, second)


def exchange(blocks, axes):
    return lax.all_to_all(blocks, axes, split_axis=0, concat_axis=0, tiled=False)


def swap(block, axis, bit=1):
    size = lax.axis_size(axis)
    return lax.ppermute(block, axis, [(i, i ^ bit) for i in range(size)])


def tie(*values):
    return lax.optimization_barrier(values)


def normalize_kernel(width, hidden_ref, out_ref, held, arrived):
    steps, rows, _ = held.shape
    parts = rows // CHUNK

    def copy(at):
        where = (at // parts, pl.ds(pl.multiple_of((at % parts) * CHUNK, CHUNK), CHUNK))
        return pltpu.make_async_copy(hidden_ref.at[(0,) + where], held.at[where], arrived.at[at])

    for at in range(steps * parts):
        copy(at).start()

    def chunk(at, carry):
        copy(at).wait()
        step, here = at // parts, pl.ds(pl.multiple_of((at % parts) * CHUNK, CHUNK), CHUNK)
        wide = held[step, here].astype(f32)
        power = jnp.mean(wide * wide, axis=-1, keepdims=True)
        normed = (wide * lax.rsqrt(power + NORM_EPS)).astype(bf16)
        for block in range(out_ref.shape[0]):
            x, zn, zf = block // 4, (block // 2) % 2, block % 2
            owner = x * 4 + zf * 2 + zn
            out_ref[block, step, here] = normed[:, owner * width : (owner + 1) * width]
        return carry

    lax.fori_loop(0, steps * parts, chunk, 0)


def normalize(hidden, shards):
    _, steps, rows, model_width = hidden.shape
    width = model_width // shards
    return pl.pallas_call(
        functools.partial(normalize_kernel, width),
        in_specs=[pl.BlockSpec(memory_space=pltpu.MemorySpace.HBM)],
        out_specs=pl.BlockSpec(memory_space=pltpu.MemorySpace.VMEM),
        out_shape=jax.ShapeDtypeStruct((shards, steps, rows, width), bf16),
        scratch_shapes=[
            pltpu.VMEM((steps, rows, model_width), bf16),
            pltpu.SemaphoreType.DMA((steps * rows // CHUNK,)),
        ],
        compiler_params=pltpu.CompilerParams(vmem_limit_bytes=VMEM),
        cost_estimate=pl.CostEstimate(
            flops=8 * rows * model_width, bytes_accessed=8 * rows * model_width, transcendentals=rows
        ),
        name="normalize",
    )(hidden)


def error_kernel(scale, own_ref, got_ref, target_ref, weight_ref, out_ref):
    tokens, columns = target_ref.shape
    weight = weight_ref[...]
    values = (own_ref[...] + got_ref[...].astype(f32)) * scale
    error = values - target_ref[...].astype(f32)
    grad = (weight * error / columns).astype(bf16)
    each = jnp.sum(error * error, axis=-1, keepdims=True) / columns
    loss = jnp.sum(weight * 0.5 * each, axis=0, keepdims=True)
    high = loss.astype(bf16).astype(f32)
    middle = (loss - high).astype(bf16).astype(f32)
    low = loss - high - middle
    lane = lax.broadcasted_iota(jnp.int32, (EXTRA, columns), 1)
    lane = lane + columns * lax.broadcasted_iota(jnp.int32, (EXTRA, columns), 0)
    row = jnp.where(lane == 0, high, jnp.where(lane == 1, middle, jnp.where(lane == 2, low, 0.0)))
    row = row.astype(bf16)
    for at in range(out_ref.shape[0]):
        out_ref[at, :tokens] = grad
        out_ref[at, tokens:] = row


def errors(own, got, target, weight, copies, scale):
    tokens, columns = target.shape
    return pl.pallas_call(
        functools.partial(error_kernel, scale),
        out_shape=jax.ShapeDtypeStruct((copies, tokens + EXTRA, columns), bf16),
        compiler_params=pltpu.CompilerParams(vmem_limit_bytes=VMEM),
        cost_estimate=pl.CostEstimate(
            flops=8 * tokens * columns, bytes_accessed=30 * tokens * columns, transcendentals=0
        ),
        name="errors",
    )(own, got, target, weight)


def finish_kernel(
    scale, got_ref, columns_ref, master_ref, first_ref, second_ref, outer_ref, start_ref, loss_ref,
    out_ref, losses_ref, everyone, done, sent,
):
    groups = got_ref.shape[0]
    features = columns_ref.shape[1]
    tokens, width = everyone.shape[0] // groups, outer_ref.shape[1]
    for at in range(groups):
        everyone[at * tokens : (at + 1) * tokens] = got_ref[at, :tokens]
    half = features // 2
    here = pl.ds(pl.multiple_of(start_ref[0], 128), width)

    def copy(at):
        rows = pl.ds(at * half, half)
        return pltpu.make_async_copy(done.at[rows], out_ref.at[0, rows], sent.at[at])

    for at in range(2):
        rows = slice(at * half, (at + 1) * half)
        gradient = scale * lax.dot_general(
            columns_ref[:, rows], everyone[...], (((0,), (0,)), ((), ())), preferred_element_type=f32
        )
        done[rows] = adam_update(master_ref[rows], first_ref[rows], second_ref[rows], gradient)[0]
        done[rows, here] = MIXING * done[rows, here] + (1.0 - MIXING) * outer_ref[rows]
        copy(at).start()
    last = jnp.sum(got_ref[:, tokens:].astype(f32), axis=0)
    last = jnp.sum(jnp.sum(last, axis=0, keepdims=True), axis=1, keepdims=True)
    lane = lax.broadcasted_iota(jnp.int32, losses_ref.shape, 1)
    losses_ref[...] = jnp.where(lane == 0, loss_ref[...], last)
    for at in range(2):
        copy(at).wait()


def finish(got, columns, master, first, second, outer, start, loss, scale):
    groups, rows, wide = got.shape
    features = columns.shape[1]
    vmem = pl.BlockSpec(memory_space=pltpu.MemorySpace.VMEM)
    return pl.pallas_call(
        functools.partial(finish_kernel, scale),
        in_specs=[vmem] * 6 + [pl.BlockSpec(memory_space=pltpu.MemorySpace.SMEM), vmem],
        out_specs=(pl.BlockSpec(memory_space=pltpu.MemorySpace.HBM), vmem),
        out_shape=(
            jax.ShapeDtypeStruct((1, features, wide), f32),
            jax.ShapeDtypeStruct((1, 2), f32),
        ),
        scratch_shapes=[
            pltpu.VMEM((groups * (rows - EXTRA), wide), bf16),
            pltpu.VMEM((features, wide), f32),
            pltpu.SemaphoreType.DMA((2,)),
        ],
        compiler_params=pltpu.CompilerParams(vmem_limit_bytes=VMEM),
        name="finish",
    )(got, columns, master, first, second, outer, start, loss)


def body(hidden, targets, doc_ids, weights, adam_m, adam_v, anchor, momentum, fragment):
    steps_total, rows, model_width = hidden.shape[1:]
    shard_rows, value_width = weights.shape[1:]
    frag_width = anchor.shape[1]
    nx, nn, nf = (lax.axis_size(a) for a in ORDER)
    shards, groups = nx * nn * nf, nx * nn
    f_at, c_at = lax.axis_index("zf"), lax.axis_index("c")
    scale = model_width ** (-0.5)
    zero = jnp.zeros((), jnp.int32)
    start = fragment[0] * frag_width
    replicas = lax.axis_size(REPLICA)
    tokens = nf * rows

    def pick(array, at, axis):
        return lax.dynamic_index_in_dim(array, at, axis, keepdims=False)

    blocks = normalize(hidden, shards)
    blocks, weights, targets, doc_ids = tie(blocks, weights, targets, doc_ids)
    columns = exchange(blocks, ORDER)

    doc_range = jnp.arange(DOCS, dtype=jnp.int32)
    counts = jnp.sum((doc_ids[0][..., None] == doc_range).astype(f32), axis=1)
    for axis, bit in (("x", 1), ("x", 2), ("zn", 1)):
        counts = counts + swap(counts, axis, bit)

    def extra_row(values):
        values = values.astype(bf16)
        return jnp.pad(values, ((0, 0), (0, value_width - values.shape[1])))[:, None]

    extra = [extra_row(doc_ids[0]), extra_row(counts)]
    extra.append(jnp.zeros((steps_total, EXTRA - len(extra), value_width), bf16))
    own_rows = jnp.concatenate([targets[0], *extra], axis=1)
    far_rows = swap(own_rows, "zf")
    pair = jnp.concatenate(
        [jnp.where(f_at == 0, own_rows, far_rows), jnp.where(f_at == 0, far_rows, own_rows)], axis=1
    )
    cuts = [at * (rows + EXTRA) for at in range(nf)]
    pair_targets = jnp.concatenate([pair[:, at : at + rows] for at in cuts], axis=1)
    pair_ids = jnp.concatenate([pair[:, at + rows, :rows] for at in cuts], axis=1).astype(jnp.int32)
    counts = counts + far_rows[:, rows + 1, :DOCS].astype(f32)
    inverse = 1.0 / (DOCS * counts)
    hot = (pair_ids[..., None] == doc_range).astype(f32)
    token_weight = jnp.sum(hot * inverse[:, None, :], axis=-1, keepdims=True)

    half = shard_rows // 2
    local = lax.dynamic_slice(weights[0], (zero, start), (shard_rows, frag_width))
    local = local.reshape(2, half, frag_width)
    summed = pick(local, c_at, 0).astype(f32) + swap(pick(local, c_at ^ 1, 0), "c").astype(f32)
    summed = summed + swap(summed, "zh")
    summed = summed + swap(summed, "y", 1)

    columns, pair_targets, token_weight, summed = tie(columns, pair_targets, token_weight, summed)

    master = weights[0].astype(f32)
    first = adam_m[0].astype(f32)
    second = adam_v[0].astype(f32)
    for step in range(steps_total):
        current = master.astype(bf16)
        rows_now = columns[:, step].reshape(shards * rows, shard_rows)
        partial = jnp.dot(rows_now, current, preferred_element_type=f32)
        partial = partial.astype(bf16).reshape(groups, tokens, value_width)
        partial = exchange(partial, GROUP)
        if step == 0:
            summed = summed + swap(summed, "y", 2)
            partial, summed = tie(partial, summed)
        else:
            other = swap(summed, "c")
            partial, summed, other = tie(partial, summed, other)
        own = jnp.sum(partial.astype(f32), axis=0)
        got = swap(own.astype(bf16), "zf")
        sent = errors(own, got, pair_targets[step], token_weight[step], groups, scale)
        if step == 0:
            sent, summed = tie(sent, summed)
        got = exchange(sent, GROUP)
        if step == 0:
            summed = summed + swap(summed, "y", 4)
            got, summed = tie(got, summed)
            loss = jnp.sum(got[:, tokens:].astype(f32)).reshape(1, 1)
            everyone = got[:, :tokens].reshape(shards * rows, value_width)
            gradient = (
                lax.dot_general(
                    rows_now, everyone, (((0,), (0,)), ((), ())), preferred_element_type=f32
                )
                * scale
            )
            master, first, second = adam_update(master, first, second, gradient)

    anchor_rows = anchor.astype(f32)
    summed = jnp.concatenate(
        [jnp.where(c_at == 0, summed, other), jnp.where(c_at == 0, other, summed)], axis=0
    )
    mean_delta = anchor_rows - summed / replicas
    new_moment = NESTEROV * momentum.astype(f32) + mean_delta
    global_fragment = anchor_rows - OUTER_RATE * (mean_delta + NESTEROV * new_moment)
    got, rows_now, master, first, second, global_fragment, loss = tie(
        got, rows_now, master, first, second, global_fragment, loss
    )
    return finish(
        got, rows_now, master, first, second, global_fragment, start.reshape(1), loss, scale
    )


def solution(mesh):
    fine = Mesh(mesh.devices.reshape(2, 8, 2, 4, 2, 2), REPLICA + FSDP)
    placed = (
        P(REPLICA, None, FSDP, None),
        P(REPLICA, None, FSDP, None),
        P(REPLICA, None, FSDP),
        P(REPLICA, FSDP, None),
        P(REPLICA, FSDP, None),
        P(REPLICA, FSDP, None),
        P(FSDP, None),
        P(FSDP, None),
        P(),
    )
    return jax.shard_map(
        body,
        mesh=fine,
        in_specs=placed,
        out_specs=(P(REPLICA, FSDP, None), P(REPLICA, None)),
        check_vma=False,
    )
```

```python
import functools

import jax
import jax.numpy as jnp
from jax import lax
from jax.experimental import pallas as pl
from jax.experimental.pallas import tpu as pltpu
from jax.sharding import Mesh, PartitionSpec as P

DOCS = 8


NORM_EPS = 1e-05
ADAM_EPS = 1e-08
INNER_RATE = 0.1
DECAY_RATE = 0.1
BETA_FIRST = 0.9
BETA_SECOND = 0.95
OUTER_RATE = 0.7
NESTEROV = 0.9
MIXING = 0.5

REPLICA = ("zh", "y", "c")
FSDP = ("x", "zf", "zn")
ORDER = ("x", "zn", "zf")
GROUP = ("x", "zn")
EXTRA = 16
CHUNK = 32
VMEM = 16 * 1024 * 1024
ALL_VMEM = 60 * 1024 * 1024

bf16, f32 = jnp.bfloat16, jnp.float32


def adam_update(master, first, second, gradient):
    first = BETA_FIRST * first + (1.0 - BETA_FIRST) * gradient
    second = BETA_SECOND * second + (1.0 - BETA_SECOND) * gradient * gradient
    master = master - INNER_RATE * (first / (jnp.sqrt(second) + ADAM_EPS) + DECAY_RATE * master)
    return (master, first, second)


def exchange(blocks, axes):
    return lax.all_to_all(blocks, axes, split_axis=0, concat_axis=0, tiled=False)


def swap(block, axis, bit=1):
    size = lax.axis_size(axis)
    return lax.ppermute(block, axis, [(i, i ^ bit) for i in range(size)])


def tie(*values):
    return lax.optimization_barrier(values)


def normalize_kernel(width, hidden_ref, out_ref, held, arrived):
    steps, rows, _ = held.shape
    parts = rows // CHUNK

    def copy(at):
        where = (at // parts, pl.ds(pl.multiple_of((at % parts) * CHUNK, CHUNK), CHUNK))
        return pltpu.make_async_copy(hidden_ref.at[(0,) + where], held.at[where], arrived.at[at])

    for at in range(steps * parts):
        copy(at).start()

    def chunk(at, carry):
        copy(at).wait()
        step, here = at // parts, pl.ds(pl.multiple_of((at % parts) * CHUNK, CHUNK), CHUNK)
        wide = held[step, here].astype(f32)
        power = jnp.mean(wide * wide, axis=-1, keepdims=True)
        normed = (wide * lax.rsqrt(power + NORM_EPS)).astype(bf16)
        for block in range(out_ref.shape[0]):
            x, zn, zf = block // 4, (block // 2) % 2, block % 2
            owner = x * 4 + zf * 2 + zn
            out_ref[block, step, here] = normed[:, owner * width : (owner + 1) * width]
        return carry

    lax.fori_loop(0, steps * parts, chunk, 0)


def normalize(hidden, shards):
    _, steps, rows, model_width = hidden.shape
    width = model_width // shards
    return pl.pallas_call(
        functools.partial(normalize_kernel, width),
        in_specs=[pl.BlockSpec(memory_space=pl.ANY)],
        out_specs=pl.BlockSpec(memory_space=pltpu.MemorySpace.VMEM),
        out_shape=jax.ShapeDtypeStruct((shards, steps, rows, width), bf16),
        scratch_shapes=[
            pltpu.VMEM((steps, rows, model_width), bf16),
            pltpu.SemaphoreType.DMA((steps * rows // CHUNK,)),
        ],
        compiler_params=pltpu.CompilerParams(vmem_limit_bytes=ALL_VMEM),
        cost_estimate=pl.CostEstimate(
            flops=8 * rows * model_width, bytes_accessed=8 * rows * model_width, transcendentals=rows
        ),
        name="normalize",
    )(hidden)


def error_kernel(scale, own_ref, got_ref, target_ref, weight_ref, out_ref):
    tokens, columns = target_ref.shape
    weight = weight_ref[...]
    values = (own_ref[...] + got_ref[...].astype(f32)) * scale
    error = values - target_ref[...].astype(f32)
    grad = (weight * error / columns).astype(bf16)
    each = jnp.sum(error * error, axis=-1, keepdims=True) / columns
    loss = jnp.sum(weight * 0.5 * each, axis=0, keepdims=True)
    high = loss.astype(bf16).astype(f32)
    middle = (loss - high).astype(bf16).astype(f32)
    low = loss - high - middle
    lane = lax.broadcasted_iota(jnp.int32, (EXTRA, columns), 1)
    lane = lane + columns * lax.broadcasted_iota(jnp.int32, (EXTRA, columns), 0)
    row = jnp.where(lane == 0, high, jnp.where(lane == 1, middle, jnp.where(lane == 2, low, 0.0)))
    row = row.astype(bf16)
    for at in range(out_ref.shape[0]):
        out_ref[at, :tokens] = grad
        out_ref[at, tokens:] = row


def errors(own, got, target, weight, copies, scale):
    tokens, columns = target.shape
    return pl.pallas_call(
        functools.partial(error_kernel, scale),
        out_shape=jax.ShapeDtypeStruct((copies, tokens + EXTRA, columns), bf16),
        compiler_params=pltpu.CompilerParams(vmem_limit_bytes=VMEM),
        cost_estimate=pl.CostEstimate(
            flops=8 * tokens * columns, bytes_accessed=30 * tokens * columns, transcendentals=0
        ),
        name="errors",
    )(own, got, target, weight)


def lay(into, blocks):
    for at, block in enumerate(blocks):
        rows = block.shape[0]
        into[at * rows : (at + 1) * rows] = block[...]


def step_rows(columns_ref, step):
    return [columns_ref.at[at, step] for at in range(columns_ref.shape[0])]


def token_rows(got_ref):
    tokens = got_ref.shape[1] - EXTRA
    return [got_ref.at[at, pl.ds(0, tokens)] for at in range(got_ref.shape[0])]


def loss_of(got_ref):
    tokens = got_ref.shape[1] - EXTRA
    total = jnp.sum(got_ref[:, tokens:].astype(f32), axis=0)
    return jnp.sum(jnp.sum(total, axis=0, keepdims=True), axis=1, keepdims=True)


def gradient_of(columns, everyone, scale):
    product = lax.dot_general(
        columns, everyone, (((0,), (0,)), ((), ())), preferred_element_type=f32
    )
    return product * scale


def project_rows(out_ref, lhs, current):
    tokens = out_ref.shape[1]
    for at in range(out_ref.shape[0]):
        rows = lhs[at * tokens : (at + 1) * tokens]
        out_ref[at] = jnp.dot(rows, current, preferred_element_type=f32).astype(bf16)


def project_kernel(columns_ref, weights_ref, out_ref, lhs, weights, sems):
    copy = pltpu.make_async_copy(weights_ref.at[0], weights, sems.at[0])
    copy.start()
    lay(lhs, step_rows(columns_ref, 0))
    copy.wait()
    project_rows(out_ref, lhs, weights[...])


def update_kernel(
    scale, got_ref, columns_ref, weights_ref, first_ref, second_ref,
    out_ref, gradient_ref, loss_ref, everyone, lhs, states, current, sems,
):
    sources = (weights_ref, first_ref, second_ref)
    copies = [
        pltpu.make_async_copy(r.at[0], states.at[at], sems.at[at]) for at, r in enumerate(sources)
    ]
    for copy in copies:
        copy.start()
    lay(everyone, token_rows(got_ref))
    lay(lhs, step_rows(columns_ref, 0))
    features = current.shape[0]
    half = features // 2
    for at in range(2):
        rows = slice(at * half, (at + 1) * half)
        gradient = gradient_of(lhs[:, rows], everyone[...], scale)
        gradient_ref[rows] = gradient
        if at == 0:
            for copy in copies:
                copy.wait()
        state = [states[k, rows].astype(f32) for k in range(3)]
        current[rows] = adam_update(*state, gradient)[0].astype(bf16)
    lay(lhs, step_rows(columns_ref, 1))
    project_rows(out_ref, lhs, current[...])
    loss_ref[...] = loss_of(got_ref)


def finish_kernel(
    scale, got_ref, columns_ref, weights_ref, first_ref, second_ref, before_ref, outer_ref, start_ref,
    loss_ref, out_ref, losses_ref, everyone, lhs, states, before, done, sems, sent,
):
    sources = (weights_ref, first_ref, second_ref)
    copies = [
        pltpu.make_async_copy(r.at[0], states.at[at], sems.at[at]) for at, r in enumerate(sources)
    ]
    copies.append(pltpu.make_async_copy(before_ref, before, sems.at[3]))
    for copy in copies:
        copy.start()
    lay(everyone, token_rows(got_ref))
    lay(lhs, step_rows(columns_ref, 1))
    features, width = done.shape[0], outer_ref.shape[1]
    half = features // 2
    here = pl.ds(pl.multiple_of(start_ref[0], 128), width)

    def give(at):
        rows = pl.ds(at * half, half)
        return pltpu.make_async_copy(done.at[rows], out_ref.at[0, rows], sent.at[at])

    for at in range(2):
        rows = slice(at * half, (at + 1) * half)
        gradient = gradient_of(lhs[:, rows], everyone[...], scale)
        if at == 0:
            for copy in copies:
                copy.wait()
        state = [states[k, rows].astype(f32) for k in range(3)]
        state = adam_update(*state, before[rows])
        done[rows] = adam_update(*state, gradient)[0]
        done[rows, here] = MIXING * done[rows, here] + (1.0 - MIXING) * outer_ref[rows]
        give(at).start()
    lane = lax.broadcasted_iota(jnp.int32, losses_ref.shape, 1)
    losses_ref[...] = jnp.where(lane == 0, loss_ref[...], loss_of(got_ref))
    for at in range(2):
        give(at).wait()


IN_VMEM = pl.BlockSpec(memory_space=pltpu.MemorySpace.VMEM)
ANYWHERE = pl.BlockSpec(memory_space=pl.ANY)


def project(columns, weights, groups):
    shards, _, rows, features = columns.shape
    tokens, wide = shards * rows, weights.shape[2]
    return pl.pallas_call(
        project_kernel,
        in_specs=[IN_VMEM, ANYWHERE],
        out_specs=IN_VMEM,
        out_shape=jax.ShapeDtypeStruct((groups, tokens // groups, wide), bf16),
        scratch_shapes=[
            pltpu.VMEM((tokens, features), bf16),
            pltpu.VMEM((features, wide), bf16),
            pltpu.SemaphoreType.DMA((1,)),
        ],
        compiler_params=pltpu.CompilerParams(vmem_limit_bytes=VMEM),
        name="project",
    )(columns, weights)


def update(got, columns, weights, first, second, scale):
    shards, _, rows, features = columns.shape
    groups, tokens, wide = got.shape[0], shards * rows, weights.shape[2]
    return pl.pallas_call(
        functools.partial(update_kernel, scale),
        in_specs=[IN_VMEM] * 2 + [ANYWHERE] * 3,
        out_specs=(IN_VMEM, IN_VMEM, IN_VMEM),
        out_shape=(
            jax.ShapeDtypeStruct((groups, tokens // groups, wide), bf16),
            jax.ShapeDtypeStruct((features, wide), f32),
            jax.ShapeDtypeStruct((1, 1), f32),
        ),
        scratch_shapes=[
            pltpu.VMEM((tokens, wide), bf16),
            pltpu.VMEM((tokens, features), bf16),
            pltpu.VMEM((3, features, wide), bf16),
            pltpu.VMEM((features, wide), bf16),
            pltpu.SemaphoreType.DMA((3,)),
        ],
        compiler_params=pltpu.CompilerParams(vmem_limit_bytes=VMEM),
        name="update",
    )(got, columns, weights, first, second)


def finish(got, columns, weights, first, second, before, outer, start, loss, scale):
    shards, _, rows, features = columns.shape
    tokens, wide = shards * rows, weights.shape[2]
    return pl.pallas_call(
        functools.partial(finish_kernel, scale),
        in_specs=[IN_VMEM] * 2
        + [ANYWHERE] * 4
        + [IN_VMEM, pl.BlockSpec(memory_space=pltpu.MemorySpace.SMEM), IN_VMEM],
        out_specs=(ANYWHERE, IN_VMEM),
        out_shape=(
            jax.ShapeDtypeStruct((1, features, wide), f32),
            jax.ShapeDtypeStruct((1, 2), f32),
        ),
        scratch_shapes=[
            pltpu.VMEM((tokens, wide), bf16),
            pltpu.VMEM((tokens, features), bf16),
            pltpu.VMEM((3, features, wide), bf16),
            pltpu.VMEM((features, wide), f32),
            pltpu.VMEM((features, wide), f32),
            pltpu.SemaphoreType.DMA((4,)),
            pltpu.SemaphoreType.DMA((2,)),
        ],
        compiler_params=pltpu.CompilerParams(vmem_limit_bytes=VMEM),
        name="finish",
    )(got, columns, weights, first, second, before, outer, start, loss)


def body(hidden, targets, doc_ids, weights, adam_m, adam_v, anchor, momentum, fragment):
    steps_total, rows, model_width = hidden.shape[1:]
    shard_rows, value_width = weights.shape[1:]
    frag_width = anchor.shape[1]
    nx, nn, nf = (lax.axis_size(a) for a in ORDER)
    shards, groups = nx * nn * nf, nx * nn
    f_at, c_at = lax.axis_index("zf"), lax.axis_index("c")
    scale = model_width ** (-0.5)
    zero = jnp.zeros((), jnp.int32)
    start = fragment[0] * frag_width
    replicas = lax.axis_size(REPLICA)
    tokens = nf * rows

    def pick(array, at, axis):
        return lax.dynamic_index_in_dim(array, at, axis, keepdims=False)

    blocks = normalize(hidden, shards)
    blocks, weights, targets, doc_ids = tie(blocks, weights, targets, doc_ids)
    columns = exchange(blocks, ORDER)

    doc_range = jnp.arange(DOCS, dtype=jnp.int32)
    counts = jnp.sum((doc_ids[0][..., None] == doc_range).astype(f32), axis=1)
    for axis, bit in (("x", 1), ("x", 2), ("zn", 1)):
        counts = counts + swap(counts, axis, bit)

    def extra_row(values):
        values = values.astype(bf16)
        return jnp.pad(values, ((0, 0), (0, value_width - values.shape[1])))[:, None]

    extra = [extra_row(doc_ids[0]), extra_row(counts)]
    extra.append(jnp.zeros((steps_total, EXTRA - len(extra), value_width), bf16))
    own_rows = jnp.concatenate([targets[0], *extra], axis=1)

    half = shard_rows // 2
    local = lax.dynamic_slice(weights[0], (zero, start), (shard_rows, frag_width))
    local = local.reshape(2, half, frag_width)
    summed = pick(local, c_at, 0).astype(f32) + swap(pick(local, c_at ^ 1, 0), "c").astype(f32)
    summed = summed + swap(summed, "y", 1)
    summed = summed + swap(summed, "y", 2)
    columns, own_rows, counts, summed = tie(columns, own_rows, counts, summed)

    partial = exchange(project(columns, weights, groups), GROUP)
    far_rows = swap(own_rows, "zf")
    pair = jnp.concatenate(
        [jnp.where(f_at == 0, own_rows, far_rows), jnp.where(f_at == 0, far_rows, own_rows)], axis=1
    )
    cuts = [at * (rows + EXTRA) for at in range(nf)]
    pair_targets = jnp.concatenate([pair[:, at : at + rows] for at in cuts], axis=1)
    pair_ids = jnp.concatenate([pair[:, at + rows, :rows] for at in cuts], axis=1).astype(jnp.int32)
    counts = counts + far_rows[:, rows + 1, :DOCS].astype(f32)
    inverse = 1.0 / (DOCS * counts)
    hot = (pair_ids[..., None] == doc_range).astype(f32)
    token_weight = jnp.sum(hot * inverse[:, None, :], axis=-1, keepdims=True)

    partial, pair_targets, token_weight, summed = tie(partial, pair_targets, token_weight, summed)

    def share_errors(partial, step):
        own = jnp.sum(partial.astype(f32), axis=0)
        got = swap(own.astype(bf16), "zf")
        return errors(own, got, pair_targets[step], token_weight[step], groups, scale)

    sent, summed = tie(share_errors(partial, 0), summed)
    got = exchange(sent, GROUP)
    summed = summed + swap(summed, "y", 4)
    got, summed = tie(got, summed)
    states = (weights, adam_m, adam_v)
    partial, gradient, loss = update(got, columns, *states, scale)
    partial, summed = tie(partial, summed)
    partial = exchange(partial, GROUP)
    summed = summed + swap(summed, "zh")
    partial, summed = tie(partial, summed)
    sent, summed = tie(share_errors(partial, 1), summed)
    got = exchange(sent, GROUP)
    other = swap(summed, "c")
    anchor_rows = anchor.astype(f32)
    summed = jnp.concatenate(
        [jnp.where(c_at == 0, summed, other), jnp.where(c_at == 0, other, summed)], axis=0
    )
    mean_delta = anchor_rows - summed / replicas
    new_moment = NESTEROV * momentum.astype(f32) + mean_delta
    global_fragment = anchor_rows - OUTER_RATE * (mean_delta + NESTEROV * new_moment)
    got, global_fragment = tie(got, global_fragment)
    return finish(
        got, columns, *states, gradient, global_fragment, start.reshape(1), loss, scale
    )


def solution(mesh):
    fine = Mesh(mesh.devices.reshape(2, 8, 2, 4, 2, 2), REPLICA + FSDP)
    placed = (
        P(REPLICA, None, FSDP, None),
        P(REPLICA, None, FSDP, None),
        P(REPLICA, None, FSDP),
        P(REPLICA, FSDP, None),
        P(REPLICA, FSDP, None),
        P(REPLICA, FSDP, None),
        P(FSDP, None),
        P(FSDP, None),
        P(),
    )
    return jax.shard_map(
        body,
        mesh=fine,
        in_specs=placed,
        out_specs=(P(REPLICA, FSDP, None), P(REPLICA, None)),
        check_vma=False,
    )
```

```python
import functools

import jax
import jax.numpy as jnp
from jax import lax
from jax.experimental import pallas as pl
from jax.experimental.pallas import tpu as pltpu
from jax.sharding import Mesh, PartitionSpec as P

DOCS = 8


NORM_EPS = 1e-05
ADAM_EPS = 1e-08
INNER_RATE = 0.1
DECAY_RATE = 0.1
BETA_FIRST = 0.9
BETA_SECOND = 0.95
OUTER_RATE = 0.7
NESTEROV = 0.9
MIXING = 0.5

REPLICA = ("zh", "y", "c")
FSDP = ("x", "zf", "zn")
ORDER = ("x", "zn", "zf")
GROUP = ("x", "zn")
EXTRA = 16
CHUNK = 32
VMEM = 60 * 1024 * 1024

bf16, f32 = jnp.bfloat16, jnp.float32


def moments(first, second, gradient):
    first = BETA_FIRST * first + (1.0 - BETA_FIRST) * gradient
    second = BETA_SECOND * second + (1.0 - BETA_SECOND) * gradient * gradient
    return (first, second)


def adam_update(master, first, second, gradient):
    first, second = moments(first, second, gradient)
    master = master - INNER_RATE * (first / (jnp.sqrt(second) + ADAM_EPS) + DECAY_RATE * master)
    return (master, first, second)


def exchange(blocks, axes):
    return lax.all_to_all(blocks, axes, split_axis=0, concat_axis=0, tiled=False)


def swap(block, axis, bit=1):
    size = lax.axis_size(axis)
    return lax.ppermute(block, axis, [(i, i ^ bit) for i in range(size)])


def tie(*values):
    return lax.optimization_barrier(values)


ANYWHERE = pl.BlockSpec(memory_space=pl.ANY)
IN_VMEM = pl.BlockSpec(memory_space=pltpu.MemorySpace.VMEM)
IN_SMEM = pl.BlockSpec(memory_space=pltpu.MemorySpace.SMEM)


def call(kernel, name, in_specs, out_specs, out_shape, scratch):
    return pl.pallas_call(
        kernel,
        in_specs=in_specs,
        out_specs=out_specs,
        out_shape=out_shape,
        scratch_shapes=scratch,
        compiler_params=pltpu.CompilerParams(vmem_limit_bytes=VMEM),
        name=name,
    )


def copies_of(pairs, sems, first=0):
    copies = [
        pltpu.make_async_copy(source, target, sems.at[first + at])
        for at, (source, target) in enumerate(pairs)
    ]
    for copy in copies:
        copy.start()
    return copies


def wait_all(copies):
    for copy in copies:
        copy.wait()


def normalize_kernel(width, hidden_ref, out_ref, held, normed, arrived, sent):
    steps, rows, _ = held.shape
    parts = rows // CHUNK

    def place(at):
        return at // parts, pl.ds(pl.multiple_of((at % parts) * CHUNK, CHUNK), CHUNK)

    def take(at):
        step, here = place(at)
        return pltpu.make_async_copy(hidden_ref.at[0, step, here], held.at[step, here], arrived.at[at])

    def give(at):
        step, here = place(at)
        return pltpu.make_async_copy(
            normed.at[:, step, here], out_ref.at[:, step, here], sent.at[at]
        )

    for at in range(steps * parts):
        take(at).start()

    def chunk(at, carry):
        take(at).wait()
        step, here = place(at)
        wide = held[step, here].astype(f32)
        power = jnp.mean(wide * wide, axis=-1, keepdims=True)
        narrow = (wide * lax.rsqrt(power + NORM_EPS)).astype(bf16)
        for block in range(out_ref.shape[0]):
            x, zn, zf = block // 4, (block // 2) % 2, block % 2
            owner = x * 4 + zf * 2 + zn
            normed[block, step, here] = narrow[:, owner * width : (owner + 1) * width]
        give(at).start()
        return carry

    lax.fori_loop(0, steps * parts, chunk, 0)
    for at in range(steps * parts):
        give(at).wait()


def normalize(hidden, shards):
    _, steps, rows, model_width = hidden.shape
    width = model_width // shards
    parts = steps * rows // CHUNK
    return call(
        functools.partial(normalize_kernel, width),
        "normalize",
        [ANYWHERE],
        ANYWHERE,
        jax.ShapeDtypeStruct((shards, steps, rows, width), bf16),
        [
            pltpu.VMEM((steps, rows, model_width), bf16),
            pltpu.VMEM((shards, steps, rows, width), bf16),
            pltpu.SemaphoreType.DMA((parts,)),
            pltpu.SemaphoreType.DMA((parts,)),
        ],
    )(hidden)


def combine_kernel(got_ref, total_ref, narrow_ref, held, sems):
    copies = copies_of([(got_ref.at[at], held.at[at]) for at in range(held.shape[0])], sems)
    total = None
    for at, copy in enumerate(copies):
        copy.wait()
        term = held[at].astype(f32)
        total = term if total is None else total + term
    total_ref[...] = total
    narrow_ref[...] = total.astype(bf16)


def combine(got):
    return call(
        combine_kernel,
        "combine",
        [ANYWHERE],
        (IN_VMEM, IN_VMEM),
        (jax.ShapeDtypeStruct(got.shape[1:], f32), jax.ShapeDtypeStruct(got.shape[1:], bf16)),
        [pltpu.VMEM(got.shape, bf16), pltpu.SemaphoreType.DMA((got.shape[0],))],
    )(got)


def error_kernel(
    scale, own_ref, got_ref, target_ref, weight_ref, out_ref, own, got, target, weight, made, sems, sent
):
    tokens, columns = target.shape
    wait_all(
        copies_of([(own_ref, own), (got_ref, got), (target_ref, target), (weight_ref, weight)], sems)
    )
    each_weight = weight[:, :1]
    values = (own[...] + got[...].astype(f32)) * scale
    error = values - target[...].astype(f32)
    made[:tokens] = (each_weight * error / columns).astype(bf16)
    each = jnp.sum(error * error, axis=-1, keepdims=True) / columns
    loss = jnp.sum(each_weight * 0.5 * each, axis=0, keepdims=True)
    high = loss.astype(bf16).astype(f32)
    middle = (loss - high).astype(bf16).astype(f32)
    low = loss - high - middle
    lane = lax.broadcasted_iota(jnp.int32, (EXTRA, columns), 1)
    lane = lane + columns * lax.broadcasted_iota(jnp.int32, (EXTRA, columns), 0)
    row = jnp.where(lane == 0, high, jnp.where(lane == 1, middle, jnp.where(lane == 2, low, 0.0)))
    made[tokens:] = row.astype(bf16)
    wait_all(copies_of([(made, out_ref.at[at]) for at in range(out_ref.shape[0])], sent))


def errors(own, got, target, weight, groups, scale):
    tokens, columns = target.shape
    return call(
        functools.partial(error_kernel, scale),
        "errors",
        [ANYWHERE] * 4,
        ANYWHERE,
        jax.ShapeDtypeStruct((groups, tokens + EXTRA, columns), bf16),
        [
            pltpu.VMEM((tokens, columns), f32),
            pltpu.VMEM((tokens, columns), bf16),
            pltpu.VMEM((tokens, columns), bf16),
            pltpu.VMEM(weight.shape, f32),
            pltpu.VMEM((tokens + EXTRA, columns), bf16),
            pltpu.SemaphoreType.DMA((4,)),
            pltpu.SemaphoreType.DMA((groups,)),
        ],
    )(own, got, target, weight)


def step_rows(columns_ref, step, into):
    rows = columns_ref.shape[2]
    return [
        (columns_ref.at[at, step], into.at[pl.ds(at * rows, rows)])
        for at in range(columns_ref.shape[0])
    ]


def token_rows(got_ref, into, extra):
    groups, tokens = got_ref.shape[0], got_ref.shape[1] - EXTRA
    pairs = [
        (got_ref.at[at, pl.ds(0, tokens)], into.at[pl.ds(at * tokens, tokens)])
        for at in range(groups)
    ]
    return pairs + [(got_ref.at[at, pl.ds(tokens, EXTRA)], extra.at[at]) for at in range(groups)]


def loss_of(extra):
    total = jnp.sum(extra[...].astype(f32), axis=0)
    return jnp.sum(jnp.sum(total, axis=0, keepdims=True), axis=1, keepdims=True)


def gradient_of(columns, everyone, scale):
    product = lax.dot_general(
        columns, everyone, (((0,), (0,)), ((), ())), preferred_element_type=f32
    )
    return product * scale


def project_rows(arriving, lhs, current, made, out_ref, sent):
    groups, tokens, _ = made.shape
    leaving, share = [], len(arriving) * 2 // groups
    for at in range(0, groups, 2):
        wait_all(arriving[at // 2 * share : (at // 2 + 1) * share])
        rows = lhs[at * tokens : (at + 2) * tokens]
        product = jnp.dot(rows, current, preferred_element_type=f32).astype(bf16)
        made[at : at + 2] = product.reshape(2, tokens, product.shape[1])
        leaving += copies_of([(made.at[pl.ds(at, 2)], out_ref.at[pl.ds(at, 2)])], sent, at // 2)
    return leaving


def project_kernel(columns_ref, weights_ref, out_ref, lhs, weights, made, sems, sent):
    (state,) = copies_of([(weights_ref.at[0], weights)], sems)
    arriving = copies_of(step_rows(columns_ref, 0, lhs), sems, 1)
    state.wait()
    wait_all(project_rows(arriving, lhs, weights[...], made, out_ref, sent))


def project(columns, weights, groups):
    shards, _, rows, features = columns.shape
    tokens, wide = shards * rows, weights.shape[2]
    return call(
        project_kernel,
        "project",
        [ANYWHERE] * 2,
        ANYWHERE,
        jax.ShapeDtypeStruct((groups, tokens // groups, wide), bf16),
        [
            pltpu.VMEM((tokens, features), bf16),
            pltpu.VMEM((features, wide), bf16),
            pltpu.VMEM((groups, tokens // groups, wide), bf16),
            pltpu.SemaphoreType.DMA((1 + shards,)),
            pltpu.SemaphoreType.DMA((groups // 2,)),
        ],
    )(columns, weights)


def update_kernel(
    scale, got_ref, columns_ref, weights_ref, first_ref, second_ref,
    out_ref, gradient_ref, master_ref, loss_ref,
    everyone, extra, lhs, later, states, gradient, master, current, made, sems, kept, sent,
):
    pairs = token_rows(got_ref, everyone, extra) + step_rows(columns_ref, 0, lhs)
    now = copies_of(pairs, sems)
    sources = (weights_ref, first_ref, second_ref)
    loads = copies_of([(r.at[0], states.at[at]) for at, r in enumerate(sources)], sems, len(now))
    arriving = copies_of(step_rows(columns_ref, 1, later), sems, len(now) + len(loads))
    wait_all(now)
    leaving = []
    half = current.shape[0] // 2
    for at in range(2):
        rows = slice(at * half, (at + 1) * half)
        here = pl.ds(at * half, half)
        slope = gradient_of(lhs[:, rows], everyone[...], scale)
        gradient[rows] = slope
        if at == 0:
            wait_all(loads)
        after = adam_update(*(states[k, rows].astype(f32) for k in range(3)), slope)[0]
        master[rows] = after
        current[rows] = after.astype(bf16)
        pairs = [(gradient.at[here], gradient_ref.at[here]), (master.at[here], master_ref.at[here])]
        leaving += copies_of(pairs, kept, 2 * at)
    leaving += project_rows(arriving, later, current[...], made, out_ref, sent)
    loss_ref[...] = loss_of(extra)
    wait_all(leaving)


def update(got, columns, weights, first, second, scale):
    shards, _, rows, features = columns.shape
    groups, tokens, wide = got.shape[0], shards * rows, weights.shape[2]
    state = jax.ShapeDtypeStruct((features, wide), f32)
    return call(
        functools.partial(update_kernel, scale),
        "update",
        [ANYWHERE] * 5,
        (ANYWHERE, ANYWHERE, ANYWHERE, IN_VMEM),
        (
            jax.ShapeDtypeStruct((groups, tokens // groups, wide), bf16),
            state,
            state,
            jax.ShapeDtypeStruct((1, 1), f32),
        ),
        [
            pltpu.VMEM((tokens, wide), bf16),
            pltpu.VMEM((groups, EXTRA, wide), bf16),
            pltpu.VMEM((tokens, features), bf16),
            pltpu.VMEM((tokens, features), bf16),
            pltpu.VMEM((3, features, wide), bf16),
            pltpu.VMEM((features, wide), f32),
            pltpu.VMEM((features, wide), f32),
            pltpu.VMEM((features, wide), bf16),
            pltpu.VMEM((groups, tokens // groups, wide), bf16),
            pltpu.SemaphoreType.DMA((2 * groups + 2 * shards + 3,)),
            pltpu.SemaphoreType.DMA((4,)),
            pltpu.SemaphoreType.DMA((groups // 2,)),
        ],
    )(got, columns, weights, first, second)


def finish_kernel(
    scale, got_ref, columns_ref, first_ref, second_ref, before_ref, master_ref, outer_ref, start_ref,
    loss_ref, out_ref, losses_ref,
    everyone, extra, lhs, states, before, master, outer, done, sems, sent,
):
    pairs = token_rows(got_ref, everyone, extra) + step_rows(columns_ref, 1, lhs)
    now = copies_of(pairs, sems)
    pairs = [(first_ref.at[0], states.at[0]), (second_ref.at[0], states.at[1])]
    pairs += [(before_ref, before), (master_ref, master), (outer_ref, outer)]
    loads = copies_of(pairs, sems, len(now))
    wait_all(now)
    features, width = done.shape[0], outer.shape[1]
    half = features // 2
    start = pl.ds(pl.multiple_of(start_ref[0], 128), width)
    leaving = []
    for at in range(2):
        rows = slice(at * half, (at + 1) * half)
        here = pl.ds(at * half, half)
        slope = gradient_of(lhs[:, rows], everyone[...], scale)
        if at == 0:
            wait_all(loads)
        first, second = moments(*(states[k, rows].astype(f32) for k in range(2)), before[rows])
        done[rows] = adam_update(master[rows], first, second, slope)[0]
        done[rows, start] = MIXING * done[rows, start] + (1.0 - MIXING) * outer[rows]
        leaving += copies_of([(done.at[here], out_ref.at[0, here])], sent, at)
    lane = lax.broadcasted_iota(jnp.int32, losses_ref.shape, 1)
    losses_ref[...] = jnp.where(lane == 0, loss_ref[...], loss_of(extra))
    wait_all(leaving)


def finish(got, columns, first, second, before, master, outer, start, loss, scale):
    shards, _, rows, features = columns.shape
    groups, tokens, wide = got.shape[0], shards * rows, first.shape[2]
    return call(
        functools.partial(finish_kernel, scale),
        "finish",
        [ANYWHERE] * 7 + [IN_SMEM, IN_VMEM],
        (ANYWHERE, IN_VMEM),
        (
            jax.ShapeDtypeStruct((1, features, wide), f32),
            jax.ShapeDtypeStruct((1, 2), f32),
        ),
        [
            pltpu.VMEM((tokens, wide), bf16),
            pltpu.VMEM((groups, EXTRA, wide), bf16),
            pltpu.VMEM((tokens, features), bf16),
            pltpu.VMEM((2, features, wide), bf16),
            pltpu.VMEM((features, wide), f32),
            pltpu.VMEM((features, wide), f32),
            pltpu.VMEM(outer.shape, f32),
            pltpu.VMEM((features, wide), f32),
            pltpu.SemaphoreType.DMA((2 * groups + shards + 5,)),
            pltpu.SemaphoreType.DMA((2,)),
        ],
    )(got, columns, first, second, before, master, outer, start, loss)


def body(hidden, targets, doc_ids, weights, adam_m, adam_v, anchor, momentum, fragment):
    steps_total, rows, model_width = hidden.shape[1:]
    shard_rows, value_width = weights.shape[1:]
    frag_width = anchor.shape[1]
    nx, nn, nf = (lax.axis_size(a) for a in ORDER)
    shards, groups = nx * nn * nf, nx * nn
    f_at, c_at = lax.axis_index("zf"), lax.axis_index("c")
    scale = model_width ** (-0.5)
    zero = jnp.zeros((), jnp.int32)
    start = fragment[0] * frag_width
    replicas = lax.axis_size(REPLICA)
    tokens = nf * rows

    def pick(array, at, axis):
        return lax.dynamic_index_in_dim(array, at, axis, keepdims=False)

    blocks = normalize(hidden, shards)
    blocks, weights, targets, doc_ids = tie(blocks, weights, targets, doc_ids)
    columns = exchange(blocks, ORDER)

    doc_range = jnp.arange(DOCS, dtype=jnp.int32)
    counts = jnp.sum((doc_ids[0][..., None] == doc_range).astype(f32), axis=1)
    for axis, bit in (("x", 1), ("x", 2), ("zn", 1)):
        counts = counts + swap(counts, axis, bit)

    def extra_row(values):
        values = values.astype(bf16)
        return jnp.pad(values, ((0, 0), (0, value_width - values.shape[1])))[:, None]

    every_count = jnp.broadcast_to(counts.reshape(1, -1), (steps_total, counts.size))
    extra = [extra_row(doc_ids[0]), extra_row(every_count)]
    extra.append(jnp.zeros((steps_total, EXTRA - len(extra), value_width), bf16))
    own_rows = jnp.concatenate([targets[0], *extra], axis=1)

    half = shard_rows // 2
    local = lax.dynamic_slice(weights[0], (zero, start), (shard_rows, frag_width))
    local = local.reshape(2, half, frag_width)
    summed = pick(local, c_at, 0).astype(f32) + swap(pick(local, c_at ^ 1, 0), "c").astype(f32)
    summed = summed + swap(summed, "zh")
    columns, own_rows, counts, summed = tie(columns, own_rows, counts, summed)

    def of_pair(own, far):
        first, last = jnp.where(f_at == 0, own, far), jnp.where(f_at == 0, far, own)
        return jnp.concatenate([first[:rows], last[:rows]]), (first[rows], last[rows])

    def weights_of(ids, inverse):
        hot = (jnp.concatenate([i[:rows] for i in ids])[:, None].astype(jnp.int32) == doc_range)
        weight = jnp.sum(hot.astype(f32) * inverse[None, :], axis=-1, keepdims=True)
        return jnp.broadcast_to(weight, (tokens, 128))

    partial = exchange(project(columns, weights, groups), GROUP)
    far_rows = swap(own_rows[0], "zf")
    summed = summed + swap(summed, "y", 1)
    far_counts = far_rows[rows + 1, : steps_total * DOCS].astype(f32)
    inverse = 1.0 / (DOCS * (counts + far_counts.reshape(counts.shape)))
    target, ids = of_pair(own_rows[0], far_rows)
    weight = weights_of(ids, inverse[0])
    partial, target, weight, summed, inverse = tie(partial, target, weight, summed, inverse)

    def share_errors(partial, target, weight):
        own, narrow = combine(partial)
        return errors(own, swap(narrow, "zf"), target, weight, groups, scale)

    sent, summed, own_rows, inverse = tie(
        share_errors(partial, target, weight), summed, own_rows, inverse
    )
    got = exchange(sent, GROUP)
    target, ids = of_pair(own_rows[1], swap(own_rows[1], "zf"))
    weight = weights_of(ids, inverse[1])
    summed = summed + swap(summed, "y", 2)
    got, summed, target, weight = tie(got, summed, target, weight)
    partial, gradient, master, loss = update(got, columns, weights, adam_m, adam_v, scale)
    partial, summed = tie(partial, summed)
    partial = exchange(partial, GROUP)
    summed = summed + swap(summed, "y", 4)
    partial, summed = tie(partial, summed)
    sent, summed = tie(share_errors(partial, target, weight), summed)
    got = exchange(sent, GROUP)
    other = swap(summed, "c")
    anchor_rows = anchor.astype(f32)
    summed = jnp.concatenate(
        [jnp.where(c_at == 0, summed, other), jnp.where(c_at == 0, other, summed)], axis=0
    )
    mean_delta = anchor_rows - summed / replicas
    new_moment = NESTEROV * momentum.astype(f32) + mean_delta
    global_fragment = anchor_rows - OUTER_RATE * (mean_delta + NESTEROV * new_moment)
    got, global_fragment = tie(got, global_fragment)
    return finish(
        got, columns, adam_m, adam_v, gradient, master, global_fragment, start.reshape(1), loss, scale
    )


def solution(mesh):
    fine = Mesh(mesh.devices.reshape(2, 8, 2, 4, 2, 2), REPLICA + FSDP)
    placed = (
        P(REPLICA, None, FSDP, None),
        P(REPLICA, None, FSDP, None),
        P(REPLICA, None, FSDP),
        P(REPLICA, FSDP, None),
        P(REPLICA, FSDP, None),
        P(REPLICA, FSDP, None),
        P(FSDP, None),
        P(FSDP, None),
        P(),
    )
    return jax.shard_map(
        body,
        mesh=fine,
        in_specs=placed,
        out_specs=(P(REPLICA, FSDP, None), P(REPLICA, None)),
        check_vma=False,
    )
```

```python
import functools

import jax
import jax.numpy as jnp
from jax import lax
from jax.experimental import pallas as pl
from jax.experimental.pallas import tpu as pltpu
from jax.sharding import Mesh, PartitionSpec as P

DOCS = 8


NORM_EPS = 1e-05
ADAM_EPS = 1e-08
INNER_RATE = 0.1
DECAY_RATE = 0.1
BETA_FIRST = 0.9
BETA_SECOND = 0.95
OUTER_RATE = 0.7
NESTEROV = 0.9
MIXING = 0.5

REPLICA = ("zh", "y", "c")
FSDP = ("x", "zf", "zn")
ORDER = ("x", "zn", "zf")
GROUP = ("x", "zn")
EXTRA = 16
CHUNK = 32
VMEM = 48 * 1024 * 1024
ALL_VMEM = 60 * 1024 * 1024

bf16, f32 = jnp.bfloat16, jnp.float32


def adam_update(master, first, second, gradient):
    first = BETA_FIRST * first + (1.0 - BETA_FIRST) * gradient
    second = BETA_SECOND * second + (1.0 - BETA_SECOND) * gradient * gradient
    master = master - INNER_RATE * (first / (jnp.sqrt(second) + ADAM_EPS) + DECAY_RATE * master)
    return (master, first, second)


def exchange(blocks, axes):
    return lax.all_to_all(blocks, axes, split_axis=0, concat_axis=0, tiled=False)


def swap(block, axis, bit=1):
    size = lax.axis_size(axis)
    return lax.ppermute(block, axis, [(i, i ^ bit) for i in range(size)])


def tie(*values):
    return lax.optimization_barrier(values)


def normalize_kernel(width, hidden_ref, out_ref, held, normed, arrived, sent):
    steps, rows, _ = held.shape
    parts = rows // CHUNK

    def place(at):
        return at // parts, pl.ds(pl.multiple_of((at % parts) * CHUNK, CHUNK), CHUNK)

    def take(at):
        step, here = place(at)
        return pltpu.make_async_copy(hidden_ref.at[0, step, here], held.at[step, here], arrived.at[at])

    def give(at):
        step, here = place(at)
        return pltpu.make_async_copy(
            normed.at[:, step, here], out_ref.at[:, step, here], sent.at[at]
        )

    for at in range(steps * parts):
        take(at).start()

    def chunk(at, carry):
        take(at).wait()
        step, here = place(at)
        wide = held[step, here].astype(f32)
        power = jnp.mean(wide * wide, axis=-1, keepdims=True)
        narrow = (wide * lax.rsqrt(power + NORM_EPS)).astype(bf16)
        for block in range(out_ref.shape[0]):
            x, zn, zf = block // 4, (block // 2) % 2, block % 2
            owner = x * 4 + zf * 2 + zn
            normed[block, step, here] = narrow[:, owner * width : (owner + 1) * width]
        give(at).start()
        return carry

    lax.fori_loop(0, steps * parts, chunk, 0)
    for at in range(steps * parts):
        give(at).wait()


def normalize(hidden, shards):
    _, steps, rows, model_width = hidden.shape
    width = model_width // shards
    parts = steps * rows // CHUNK
    return pl.pallas_call(
        functools.partial(normalize_kernel, width),
        in_specs=[pl.BlockSpec(memory_space=pl.ANY)],
        out_specs=pl.BlockSpec(memory_space=pl.ANY),
        out_shape=jax.ShapeDtypeStruct((shards, steps, rows, width), bf16),
        scratch_shapes=[
            pltpu.VMEM((steps, rows, model_width), bf16),
            pltpu.VMEM((shards, steps, rows, width), bf16),
            pltpu.SemaphoreType.DMA((parts,)),
            pltpu.SemaphoreType.DMA((parts,)),
        ],
        compiler_params=pltpu.CompilerParams(vmem_limit_bytes=ALL_VMEM),
        name="normalize",
    )(hidden)


def error_kernel(scale, own_ref, got_ref, weight_ref, out_ref):
    tokens, columns = own_ref.shape
    weight = weight_ref[...]
    error = (own_ref[...] + got_ref[...].astype(f32)) * scale
    grad = (weight * error / columns).astype(bf16)
    each = jnp.sum(error * error, axis=-1, keepdims=True) / columns
    loss = jnp.sum(weight * 0.5 * each, axis=0, keepdims=True)
    high = loss.astype(bf16).astype(f32)
    middle = (loss - high).astype(bf16).astype(f32)
    low = loss - high - middle
    lane = lax.broadcasted_iota(jnp.int32, (EXTRA, columns), 1)
    lane = lane + columns * lax.broadcasted_iota(jnp.int32, (EXTRA, columns), 0)
    row = jnp.where(lane == 0, high, jnp.where(lane == 1, middle, jnp.where(lane == 2, low, 0.0)))
    row = row.astype(bf16)
    for at in range(out_ref.shape[0]):
        out_ref[at, :tokens] = grad
        out_ref[at, tokens:] = row


def errors(own, got, weight, copies, scale):
    tokens, columns = own.shape
    return pl.pallas_call(
        functools.partial(error_kernel, scale),
        out_shape=jax.ShapeDtypeStruct((copies, tokens + EXTRA, columns), bf16),
        compiler_params=pltpu.CompilerParams(vmem_limit_bytes=VMEM),
        cost_estimate=pl.CostEstimate(
            flops=8 * tokens * columns, bytes_accessed=30 * tokens * columns, transcendentals=0
        ),
        name="errors",
    )(own, got, weight)


def body(hidden, targets, doc_ids, weights, adam_m, adam_v, anchor, momentum, fragment):
    steps_total, rows, model_width = hidden.shape[1:]
    shard_rows, value_width = weights.shape[1:]
    frag_width = anchor.shape[1]
    nx, nn, nf = (lax.axis_size(a) for a in ORDER)
    shards, groups = nx * nn * nf, nx * nn
    f_at, c_at = lax.axis_index("zf"), lax.axis_index("c")
    scale = model_width ** (-0.5)
    zero = jnp.zeros((), jnp.int32)
    start = fragment[0] * frag_width
    replicas = lax.axis_size(REPLICA)
    tokens = nf * rows

    def pick(array, at, axis):
        return lax.dynamic_index_in_dim(array, at, axis, keepdims=False)

    blocks = normalize(hidden, shards)
    blocks, weights, targets, doc_ids = tie(blocks, weights, targets, doc_ids)
    columns = exchange(blocks, ORDER)

    doc_range = jnp.arange(DOCS, dtype=jnp.int32)
    counts = jnp.sum((doc_ids[0][..., None] == doc_range).astype(f32), axis=1)
    for axis, bit in (("x", 1), ("x", 2), ("zn", 1)):
        counts = counts + swap(counts, axis, bit)
    own_row = jnp.concatenate([doc_ids[0].astype(f32), counts], axis=1)
    own_row = jnp.pad(own_row, ((0, 0), (0, 128 - own_row.shape[1])))
    far_row = swap(own_row, "zf")
    pair = [jnp.where(f_at == 0, own_row, far_row), jnp.where(f_at == 0, far_row, own_row)]
    pair_ids = jnp.concatenate([row[:, :rows] for row in pair], axis=1).astype(jnp.int32)
    inverse = 1.0 / (DOCS * (counts + far_row[:, rows : rows + DOCS]))
    hot = (pair_ids[..., None] == doc_range).astype(f32)
    token_weight = jnp.sum(hot * inverse[:, None, :], axis=-1, keepdims=True)

    goal = targets[0].astype(f32) / scale
    goal = jnp.concatenate([jnp.where(f_at == at, goal, 0.0) for at in range(nf)], axis=1)

    half = shard_rows // 2
    local = lax.dynamic_slice(weights[0], (zero, start), (shard_rows, frag_width))
    local = local.reshape(2, half, frag_width)
    summed = pick(local, c_at, 0).astype(f32) + swap(pick(local, c_at ^ 1, 0), "c").astype(f32)
    summed = summed + swap(summed, "y", 1)

    columns, goal, token_weight, summed = tie(columns, goal, token_weight, summed)

    master = weights[0].astype(f32)
    first = adam_m[0].astype(f32)
    second = adam_v[0].astype(f32)
    loss_rows = []
    for step in range(steps_total):
        current = master.astype(bf16)
        rows_now = columns[:, step].reshape(shards * rows, shard_rows)
        partial = jnp.dot(rows_now, current, preferred_element_type=f32)
        partial = partial.astype(bf16).reshape(groups, tokens, value_width)
        partial, summed = tie(partial, summed)
        partial = exchange(partial, GROUP)
        summed = summed + (swap(summed, "y", 2) if step == 0 else swap(summed, "zh"))
        partial, summed = tie(partial, summed)
        own = jnp.sum(partial.astype(f32), axis=0) - goal[step]
        got = swap(own.astype(bf16), "zf")
        sent = errors(own, got, token_weight[step], groups, scale)
        sent, summed = tie(sent, summed)
        got = exchange(sent, GROUP)
        if step == 0:
            summed = summed + swap(summed, "y", 4)
            got, summed = tie(got, summed)
        else:
            other = swap(summed, "c")
            got, summed, other = tie(got, summed, other)
        loss_rows.append(got[:, tokens, :128])
        everyone = got[:, :tokens].reshape(shards * rows, value_width)
        gradient = (
            lax.dot_general(
                rows_now, everyone, (((0,), (0,)), ((), ())), preferred_element_type=f32
            )
            * scale
        )
        master, first, second = adam_update(master, first, second, gradient)

    anchor_rows = anchor.astype(f32)
    summed = jnp.concatenate(
        [jnp.where(c_at == 0, summed, other), jnp.where(c_at == 0, other, summed)], axis=0
    )
    mean_delta = anchor_rows - summed / replicas
    new_moment = NESTEROV * momentum.astype(f32) + mean_delta
    global_fragment = anchor_rows - OUTER_RATE * (mean_delta + NESTEROV * new_moment)
    merged = (
        MIXING * lax.dynamic_slice(master, (zero, start), (shard_rows, frag_width))
        + (1.0 - MIXING) * global_fragment
    )
    master = lax.dynamic_update_slice(master, merged, (zero, start))
    losses = jnp.sum(jnp.stack(loss_rows).astype(f32), axis=(1, 2))
    return (master[None], losses[None])


def solution(mesh):
    fine = Mesh(mesh.devices.reshape(2, 8, 2, 4, 2, 2), REPLICA + FSDP)
    placed = (
        P(REPLICA, None, FSDP, None),
        P(REPLICA, None, FSDP, None),
        P(REPLICA, None, FSDP),
        P(REPLICA, FSDP, None),
        P(REPLICA, FSDP, None),
        P(REPLICA, FSDP, None),
        P(FSDP, None),
        P(FSDP, None),
        P(),
    )
    return jax.shard_map(
        body,
        mesh=fine,
        in_specs=placed,
        out_specs=(P(REPLICA, FSDP, None), P(REPLICA, None)),
        check_vma=False,
    )
```

```python
import functools

import jax
import jax.numpy as jnp
from jax import lax
from jax.experimental import pallas as pl
from jax.experimental.pallas import tpu as pltpu
from jax.sharding import Mesh, PartitionSpec as P

DOCS = 8


NORM_EPS = 1e-05
ADAM_EPS = 1e-08
INNER_RATE = 0.1
DECAY_RATE = 0.1
BETA_FIRST = 0.9
BETA_SECOND = 0.95
OUTER_RATE = 0.7
NESTEROV = 0.9
MIXING = 0.5

REPLICA = ("zh", "y", "c")
FSDP = ("x", "zf", "zn")
ORDER = ("x", "zn", "zf")
GROUP = ("x", "zn")
EXTRA = 16
CHUNK = 32
VMEM = 8 * 1024 * 1024
ALL_VMEM = 60 * 1024 * 1024

bf16, f32 = jnp.bfloat16, jnp.float32


def adam_update(master, first, second, gradient):
    first = BETA_FIRST * first + (1.0 - BETA_FIRST) * gradient
    second = BETA_SECOND * second + (1.0 - BETA_SECOND) * gradient * gradient
    master = master - INNER_RATE * (first / (jnp.sqrt(second) + ADAM_EPS) + DECAY_RATE * master)
    return (master, first, second)


def exchange(blocks, axes):
    return lax.all_to_all(blocks, axes, split_axis=0, concat_axis=0, tiled=False)


def swap(block, axis, bit=1):
    size = lax.axis_size(axis)
    return lax.ppermute(block, axis, [(i, i ^ bit) for i in range(size)])


def tie(*values):
    return lax.optimization_barrier(values)


def normalize_kernel(width, hidden_ref, out_ref, held, normed, arrived, sent):
    steps, rows, _ = held.shape
    parts = rows // CHUNK

    def place(at):
        return at // parts, pl.ds(pl.multiple_of((at % parts) * CHUNK, CHUNK), CHUNK)

    def take(at):
        step, here = place(at)
        return pltpu.make_async_copy(hidden_ref.at[0, step, here], held.at[step, here], arrived.at[at])

    def give(at):
        step, here = place(at)
        return pltpu.make_async_copy(
            normed.at[:, step, here], out_ref.at[:, step, here], sent.at[at]
        )

    for at in range(steps * parts):
        take(at).start()

    def chunk(at, carry):
        take(at).wait()
        step, here = place(at)
        wide = held[step, here].astype(f32)
        power = jnp.mean(wide * wide, axis=-1, keepdims=True)
        narrow = (wide * lax.rsqrt(power + NORM_EPS)).astype(bf16)
        for block in range(out_ref.shape[0]):
            x, zn, zf = block // 4, (block // 2) % 2, block % 2
            owner = x * 4 + zf * 2 + zn
            normed[block, step, here] = narrow[:, owner * width : (owner + 1) * width]
        give(at).start()
        return carry

    lax.fori_loop(0, steps * parts, chunk, 0)
    for at in range(steps * parts):
        give(at).wait()


def normalize(hidden, shards):
    _, steps, rows, model_width = hidden.shape
    width = model_width // shards
    parts = steps * rows // CHUNK
    return pl.pallas_call(
        functools.partial(normalize_kernel, width),
        in_specs=[pl.BlockSpec(memory_space=pl.ANY)],
        out_specs=pl.BlockSpec(memory_space=pl.ANY),
        out_shape=jax.ShapeDtypeStruct((shards, steps, rows, width), bf16),
        scratch_shapes=[
            pltpu.VMEM((steps, rows, model_width), bf16),
            pltpu.VMEM((shards, steps, rows, width), bf16),
            pltpu.SemaphoreType.DMA((parts,)),
            pltpu.SemaphoreType.DMA((parts,)),
        ],
        compiler_params=pltpu.CompilerParams(vmem_limit_bytes=ALL_VMEM),
        name="normalize",
    )(hidden)


def error_kernel(scale, counted, own_ref, got_ref, hot_ref, *rest):
    tokens, columns = hot_ref.shape[0], own_ref.shape[1]
    total = own_ref[...] + got_ref[...].astype(f32)
    if counted:
        out_ref, inverse_ref = rest
        counts = total[tokens : tokens + 1, :128]
        inverse = jnp.where(counts > 0.0, 1.0 / (DOCS * jnp.maximum(counts, 1.0)), 0.0)
        inverse_ref[...] = jnp.broadcast_to(inverse, inverse_ref.shape)
    else:
        inverse_in_ref, out_ref = rest
        inverse = inverse_in_ref[:1]
    weight = jnp.sum(hot_ref[...] * inverse, axis=-1, keepdims=True)
    error = total[:tokens] * scale
    grad = (weight * error / columns).astype(bf16)
    each = jnp.sum(error * error, axis=-1, keepdims=True) / columns
    loss = jnp.sum(weight * 0.5 * each, axis=0, keepdims=True)
    high = loss.astype(bf16).astype(f32)
    middle = (loss - high).astype(bf16).astype(f32)
    low = loss - high - middle
    lane = lax.broadcasted_iota(jnp.int32, (EXTRA, columns), 1)
    lane = lane + columns * lax.broadcasted_iota(jnp.int32, (EXTRA, columns), 0)
    row = jnp.where(lane == 0, high, jnp.where(lane == 1, middle, jnp.where(lane == 2, low, 0.0)))
    row = row.astype(bf16)
    for at in range(out_ref.shape[0]):
        out_ref[at, :tokens] = grad
        out_ref[at, tokens:] = row


def errors(own, got, hot, inverse, copies, scale):
    tokens, columns = hot.shape[0], own.shape[1]
    sent = jax.ShapeDtypeStruct((copies, tokens + EXTRA, columns), bf16)
    kept = jax.ShapeDtypeStruct((8, 128), f32)
    counted = inverse is None
    return pl.pallas_call(
        functools.partial(error_kernel, scale, counted),
        out_shape=(sent, kept) if counted else sent,
        compiler_params=pltpu.CompilerParams(vmem_limit_bytes=VMEM),
        cost_estimate=pl.CostEstimate(
            flops=8 * tokens * columns, bytes_accessed=30 * tokens * columns, transcendentals=0
        ),
        name="errors",
    )(own, got, hot, *(() if counted else (inverse,)))


def project_kernel(columns_ref, weights_ref, counts_ref, out_ref, first_ref, later_ref, made, sent):
    shards, _, rows, _ = columns_ref.shape
    groups, tokens, _ = made.shape
    tokens = tokens - EXTRA
    share = tokens // rows

    def give(at):
        return pltpu.make_async_copy(made.at[pl.ds(at, 2)], out_ref.at[pl.ds(at, 2)], sent.at[at // 2])

    for at in range(0, groups, 2):
        for shard in range(at * share, (at + 2) * share):
            first_ref[shard * rows : (shard + 1) * rows] = columns_ref[shard, 0]
        product = jnp.dot(
            first_ref[at * tokens : (at + 2) * tokens], weights_ref[0], preferred_element_type=f32
        ).astype(bf16)
        for group in range(2):
            made[at + group, :tokens] = product[group * tokens : (group + 1) * tokens]
            made[at + group, tokens:] = counts_ref[...]
        give(at).start()
    for shard in range(shards):
        later_ref[shard * rows : (shard + 1) * rows] = columns_ref[shard, 1]
    for at in range(0, groups, 2):
        give(at).wait()


def project(columns, weights, count_rows, groups):
    shards, _, rows, features = columns.shape
    tokens, wide = shards * rows, weights.shape[2]
    block = jax.ShapeDtypeStruct((groups, tokens // groups + EXTRA, wide), bf16)
    plain = jax.ShapeDtypeStruct((tokens, features), bf16)
    vmem = pl.BlockSpec(memory_space=pltpu.MemorySpace.VMEM)
    return pl.pallas_call(
        project_kernel,
        in_specs=[vmem, vmem, vmem],
        out_specs=(pl.BlockSpec(memory_space=pl.ANY), vmem, vmem),
        out_shape=(block, plain, plain),
        scratch_shapes=[pltpu.VMEM(block.shape, bf16), pltpu.SemaphoreType.DMA((groups // 2,))],
        compiler_params=pltpu.CompilerParams(vmem_limit_bytes=VMEM),
        name="project",
    )(columns, weights, count_rows)


def body(hidden, targets, doc_ids, weights, adam_m, adam_v, anchor, momentum, fragment):
    steps_total, rows, model_width = hidden.shape[1:]
    shard_rows, value_width = weights.shape[1:]
    frag_width = anchor.shape[1]
    nx, nn, nf = (lax.axis_size(a) for a in ORDER)
    shards, groups = nx * nn * nf, nx * nn
    f_at, c_at = lax.axis_index("zf"), lax.axis_index("c")
    scale = model_width ** (-0.5)
    zero = jnp.zeros((), jnp.int32)
    start = fragment[0] * frag_width
    replicas = lax.axis_size(REPLICA)
    tokens = nf * rows

    def pick(array, at, axis):
        return lax.dynamic_index_in_dim(array, at, axis, keepdims=False)

    blocks = normalize(hidden, shards)
    blocks, weights, targets, doc_ids = tie(blocks, weights, targets, doc_ids)
    columns = exchange(blocks, ORDER)

    doc_range = jnp.arange(DOCS, dtype=jnp.int32)
    counts = jnp.sum((doc_ids[0][..., None] == doc_range).astype(f32), axis=1)
    count_rows = jnp.pad(
        counts.reshape(1, -1).astype(bf16),
        ((0, EXTRA - 1), (0, value_width - steps_total * DOCS)),
    )
    far_ids = swap(doc_ids[0], "zf")
    pair_ids = jnp.concatenate(
        [jnp.where(f_at == 0, doc_ids[0], far_ids), jnp.where(f_at == 0, far_ids, doc_ids[0])],
        axis=1,
    )
    step_shift = DOCS * jnp.arange(steps_total, dtype=jnp.int32)[:, None, None]
    hot = (pair_ids[..., None] + step_shift == jnp.arange(128, dtype=jnp.int32)).astype(f32)
    hot = [hot[step] for step in range(steps_total)]

    goal = targets[0].astype(f32) / scale
    goal = jnp.concatenate([jnp.where(f_at == at, goal, 0.0) for at in range(nf)], axis=1)
    goal = [jnp.pad(goal[0], ((0, EXTRA), (0, 0))), goal[1]]

    half = shard_rows // 2
    local = lax.dynamic_slice(weights[0], (zero, start), (shard_rows, frag_width))
    local = local.reshape(2, half, frag_width)
    summed = pick(local, c_at, 0).astype(f32) + swap(pick(local, c_at ^ 1, 0), "c").astype(f32)
    for bit in (1, 2, 4):
        summed = summed + swap(summed, "y", bit)

    columns, goal, hot, count_rows, summed = tie(columns, goal, hot, count_rows, summed)
    partial, *step_rows = project(columns, weights, count_rows, groups)

    master = weights[0].astype(f32)
    first = adam_m[0].astype(f32)
    second = adam_v[0].astype(f32)
    loss_rows, inverse = [], None
    for step in range(steps_total):
        rows_now = step_rows[step]
        if step == 1:
            partial = jnp.dot(rows_now, master.astype(bf16), preferred_element_type=f32)
            partial = partial.astype(bf16).reshape(groups, tokens, value_width)
            partial, summed = tie(partial, summed)
        partial = exchange(partial, GROUP)
        if step == 1:
            other = swap(summed, "c")
            partial, summed, other = tie(partial, summed, other)
        own = jnp.sum(partial.astype(f32), axis=0) - goal[step]
        got = swap(own.astype(bf16), "zf")
        sent = errors(own, got, hot[step], inverse, groups, scale)
        if step == 0:
            sent, inverse = sent
            sent, summed = tie(sent, summed)
        got = exchange(sent, GROUP)
        if step == 0:
            summed = summed + swap(summed, "zh")
            got, summed = tie(got, summed)
        loss_rows.append(got[:, tokens, :128])
        everyone = got[:, :tokens].reshape(shards * rows, value_width)
        gradient = (
            lax.dot_general(
                rows_now, everyone, (((0,), (0,)), ((), ())), preferred_element_type=f32
            )
            * scale
        )
        master, first, second = adam_update(master, first, second, gradient)

    anchor_rows = anchor.astype(f32)
    summed = jnp.concatenate(
        [jnp.where(c_at == 0, summed, other), jnp.where(c_at == 0, other, summed)], axis=0
    )
    mean_delta = anchor_rows - summed / replicas
    new_moment = NESTEROV * momentum.astype(f32) + mean_delta
    global_fragment = anchor_rows - OUTER_RATE * (mean_delta + NESTEROV * new_moment)
    merged = (
        MIXING * lax.dynamic_slice(master, (zero, start), (shard_rows, frag_width))
        + (1.0 - MIXING) * global_fragment
    )
    master = lax.dynamic_update_slice(master, merged, (zero, start))
    losses = jnp.sum(jnp.stack(loss_rows).astype(f32), axis=(1, 2))
    return (master[None], losses[None])


def solution(mesh):
    fine = Mesh(mesh.devices.reshape(2, 8, 2, 4, 2, 2), REPLICA + FSDP)
    placed = (
        P(REPLICA, None, FSDP, None),
        P(REPLICA, None, FSDP, None),
        P(REPLICA, None, FSDP),
        P(REPLICA, FSDP, None),
        P(REPLICA, FSDP, None),
        P(REPLICA, FSDP, None),
        P(FSDP, None),
        P(FSDP, None),
        P(),
    )
    return jax.shard_map(
        body,
        mesh=fine,
        in_specs=placed,
        out_specs=(P(REPLICA, FSDP, None), P(REPLICA, None)),
        check_vma=False,
    )
```

```python
import functools

import jax
import jax.numpy as jnp
from jax import lax
from jax.experimental import pallas as pl
from jax.experimental.pallas import tpu as pltpu
from jax.sharding import Mesh, PartitionSpec as P

DOCS = 8


NORM_EPS = 1e-05
ADAM_EPS = 1e-08
INNER_RATE = 0.1
DECAY_RATE = 0.1
BETA_FIRST = 0.9
BETA_SECOND = 0.95
OUTER_RATE = 0.7
NESTEROV = 0.9
MIXING = 0.5

REPLICA = ("zh", "y", "c")
FSDP = ("x", "zf", "zn")
ORDER = ("x", "zn", "zf")
GROUP = ("x", "zn")
EXTRA = 16
CHUNK = 32
VMEM = 48 * 1024 * 1024
ALL_VMEM = 60 * 1024 * 1024

bf16, f32 = jnp.bfloat16, jnp.float32


def adam_update(master, first, second, gradient):
    first = BETA_FIRST * first + (1.0 - BETA_FIRST) * gradient
    second = BETA_SECOND * second + (1.0 - BETA_SECOND) * gradient * gradient
    master = master - INNER_RATE * (first / (jnp.sqrt(second) + ADAM_EPS) + DECAY_RATE * master)
    return (master, first, second)


def exchange(blocks, axes):
    return lax.all_to_all(blocks, axes, split_axis=0, concat_axis=0, tiled=False)


def swap(block, axis, bit=1):
    size = lax.axis_size(axis)
    return lax.ppermute(block, axis, [(i, i ^ bit) for i in range(size)])


def tie(*values):
    return lax.optimization_barrier(values)


def normalize_kernel(width, hidden_ref, out_ref, held, normed, arrived, sent):
    steps, rows, _ = held.shape
    parts = rows // CHUNK

    def place(at):
        return at // parts, pl.ds(pl.multiple_of((at % parts) * CHUNK, CHUNK), CHUNK)

    def take(at):
        step, here = place(at)
        return pltpu.make_async_copy(hidden_ref.at[0, step, here], held.at[step, here], arrived.at[at])

    def give(at):
        step, here = place(at)
        return pltpu.make_async_copy(
            normed.at[:, step, here], out_ref.at[:, step, here], sent.at[at]
        )

    for at in range(steps * parts):
        take(at).start()

    def chunk(at, carry):
        take(at).wait()
        step, here = place(at)
        wide = held[step, here].astype(f32)
        power = jnp.mean(wide * wide, axis=-1, keepdims=True)
        narrow = (wide * lax.rsqrt(power + NORM_EPS)).astype(bf16)
        for block in range(out_ref.shape[0]):
            x, zn, zf = block // 4, (block // 2) % 2, block % 2
            owner = x * 4 + zf * 2 + zn
            normed[block, step, here] = narrow[:, owner * width : (owner + 1) * width]
        give(at).start()
        return carry

    lax.fori_loop(0, steps * parts, chunk, 0)
    for at in range(steps * parts):
        give(at).wait()


def normalize(hidden, shards):
    _, steps, rows, model_width = hidden.shape
    width = model_width // shards
    parts = steps * rows // CHUNK
    return pl.pallas_call(
        functools.partial(normalize_kernel, width),
        in_specs=[pl.BlockSpec(memory_space=pl.ANY)],
        out_specs=pl.BlockSpec(memory_space=pl.ANY),
        out_shape=jax.ShapeDtypeStruct((shards, steps, rows, width), bf16),
        scratch_shapes=[
            pltpu.VMEM((steps, rows, model_width), bf16),
            pltpu.VMEM((shards, steps, rows, width), bf16),
            pltpu.SemaphoreType.DMA((parts,)),
            pltpu.SemaphoreType.DMA((parts,)),
        ],
        compiler_params=pltpu.CompilerParams(vmem_limit_bytes=ALL_VMEM),
        name="normalize",
    )(hidden)


def error_kernel(scale, counted, own_ref, got_ref, *rest):
    tokens, columns = 128, own_ref.shape[1]
    total = own_ref[...] + got_ref[...].astype(f32)
    if counted:
        out_ref, later_ref = rest
        counts = total[tokens : tokens + 1, :128]
        inverse = jnp.where(counts > 0.0, 1.0 / (DOCS * jnp.maximum(counts, 1.0)), 0.0)
        lane = lax.broadcasted_iota(jnp.int32, (tokens, 128), 1)
        here = lane == lax.broadcasted_iota(jnp.int32, (tokens, 128), 0)
        weights = []
        for step in range(2):
            ids = jnp.where(here, total[tokens + 1 + step : tokens + 2 + step, :128], 0.0)
            ids = jnp.sum(ids, axis=-1, keepdims=True).astype(jnp.int32) + DOCS * step
            hot = jnp.where(lane == ids, inverse, 0.0)
            weights.append(jnp.sum(hot, axis=-1, keepdims=True))
        weight = weights[0]
        later_ref[...] = jnp.broadcast_to(weights[1], later_ref.shape)
    else:
        weight_ref, out_ref = rest
        weight = weight_ref[:, :1]
    error = total[:tokens] * scale
    grad = (weight * error / columns).astype(bf16)
    each = jnp.sum(error * error, axis=-1, keepdims=True) / columns
    loss = jnp.sum(weight * 0.5 * each, axis=0, keepdims=True)
    high = loss.astype(bf16).astype(f32)
    middle = (loss - high).astype(bf16).astype(f32)
    low = loss - high - middle
    lane = lax.broadcasted_iota(jnp.int32, (EXTRA, columns), 1)
    lane = lane + columns * lax.broadcasted_iota(jnp.int32, (EXTRA, columns), 0)
    row = jnp.where(lane == 0, high, jnp.where(lane == 1, middle, jnp.where(lane == 2, low, 0.0)))
    row = row.astype(bf16)
    for at in range(out_ref.shape[0]):
        out_ref[at, :tokens] = grad
        out_ref[at, tokens:] = row


def errors(own, got, weight, tokens, copies, scale):
    columns = own.shape[1]
    sent = jax.ShapeDtypeStruct((copies, tokens + EXTRA, columns), bf16)
    kept = jax.ShapeDtypeStruct((tokens, 128), f32)
    counted = weight is None
    return pl.pallas_call(
        functools.partial(error_kernel, scale, counted),
        out_shape=(sent, kept) if counted else sent,
        compiler_params=pltpu.CompilerParams(vmem_limit_bytes=VMEM),
        cost_estimate=pl.CostEstimate(
            flops=8 * tokens * columns, bytes_accessed=30 * tokens * columns, transcendentals=0
        ),
        name="errors",
    )(own, got, *(() if counted else (weight,)))


def project_kernel(columns_ref, weights_ref, counts_ref, out_ref, first_ref, later_ref, made, sent):
    shards, _, rows, _ = columns_ref.shape
    groups, tokens, _ = made.shape
    tokens = tokens - EXTRA
    share = tokens // rows

    def give(at):
        return pltpu.make_async_copy(made.at[pl.ds(at, 2)], out_ref.at[pl.ds(at, 2)], sent.at[at // 2])

    for at in range(0, groups, 2):
        for shard in range(at * share, (at + 2) * share):
            first_ref[shard * rows : (shard + 1) * rows] = columns_ref[shard, 0]
        product = jnp.dot(
            first_ref[at * tokens : (at + 2) * tokens], weights_ref[0], preferred_element_type=f32
        ).astype(bf16)
        for group in range(2):
            made[at + group, :tokens] = product[group * tokens : (group + 1) * tokens]
            made[at + group, tokens:] = counts_ref[...]
        give(at).start()
    for shard in range(shards):
        later_ref[shard * rows : (shard + 1) * rows] = columns_ref[shard, 1]
    for at in range(0, groups, 2):
        give(at).wait()


def project(columns, weights, count_rows, groups):
    shards, _, rows, features = columns.shape
    tokens, wide = shards * rows, weights.shape[2]
    block = jax.ShapeDtypeStruct((groups, tokens // groups + EXTRA, wide), bf16)
    plain = jax.ShapeDtypeStruct((tokens, features), bf16)
    vmem = pl.BlockSpec(memory_space=pltpu.MemorySpace.VMEM)
    return pl.pallas_call(
        project_kernel,
        in_specs=[vmem, vmem, vmem],
        out_specs=(pl.BlockSpec(memory_space=pl.ANY), vmem, vmem),
        out_shape=(block, plain, plain),
        scratch_shapes=[pltpu.VMEM(block.shape, bf16), pltpu.SemaphoreType.DMA((groups // 2,))],
        compiler_params=pltpu.CompilerParams(vmem_limit_bytes=VMEM),
        name="project",
    )(columns, weights, count_rows)


def body(hidden, targets, doc_ids, weights, adam_m, adam_v, anchor, momentum, fragment):
    steps_total, rows, model_width = hidden.shape[1:]
    shard_rows, value_width = weights.shape[1:]
    frag_width = anchor.shape[1]
    nx, nn, nf = (lax.axis_size(a) for a in ORDER)
    shards, groups = nx * nn * nf, nx * nn
    f_at, c_at = lax.axis_index("zf"), lax.axis_index("c")
    scale = model_width ** (-0.5)
    zero = jnp.zeros((), jnp.int32)
    start = fragment[0] * frag_width
    replicas = lax.axis_size(REPLICA)
    tokens = nf * rows

    def pick(array, at, axis):
        return lax.dynamic_index_in_dim(array, at, axis, keepdims=False)

    blocks = normalize(hidden, shards)
    blocks, weights, targets, doc_ids = tie(blocks, weights, targets, doc_ids)
    columns = exchange(blocks, ORDER)

    doc_range = jnp.arange(DOCS, dtype=jnp.int32)
    counts = jnp.sum((doc_ids[0][..., None] == doc_range).astype(f32), axis=1)
    count_rows = jnp.pad(
        counts.reshape(1, -1).astype(bf16),
        ((0, EXTRA - 1), (0, value_width - steps_total * DOCS)),
    )
    goal = targets[0].astype(f32) / scale
    goal = jnp.concatenate([jnp.where(f_at == at, goal, 0.0) for at in range(nf)], axis=1)
    ids = doc_ids[0].astype(f32)
    ids = jnp.concatenate([jnp.where(f_at == at, ids, 0.0) for at in range(nf)], axis=1)
    ids = jnp.pad(ids, ((1, EXTRA - 1 - steps_total), (0, value_width - tokens)))
    goal = [jnp.concatenate([goal[0], -ids], axis=0), goal[1]]

    half = shard_rows // 2
    local = lax.dynamic_slice(weights[0], (zero, start), (shard_rows, frag_width))
    local = local.reshape(2, half, frag_width)
    summed = pick(local, c_at, 0).astype(f32) + swap(pick(local, c_at ^ 1, 0), "c").astype(f32)
    for bit in (1, 2, 4):
        summed = summed + swap(summed, "y", bit)

    columns, goal, count_rows, summed = tie(columns, goal, count_rows, summed)
    partial, *step_rows = project(columns, weights, count_rows, groups)

    master = weights[0].astype(f32)
    first = adam_m[0].astype(f32)
    second = adam_v[0].astype(f32)
    loss_rows, weight = [], None
    for step in range(steps_total):
        rows_now = step_rows[step]
        if step == 1:
            partial = jnp.dot(rows_now, master.astype(bf16), preferred_element_type=f32)
            partial = partial.astype(bf16).reshape(groups, tokens, value_width)
            partial, summed = tie(partial, summed)
        partial = exchange(partial, GROUP)
        if step == 1:
            other = swap(summed, "c")
            partial, summed, other = tie(partial, summed, other)
        own = jnp.sum(partial.astype(f32), axis=0) - goal[step]
        got = swap(own.astype(bf16), "zf")
        sent = errors(own, got, weight, tokens, groups, scale)
        if step == 0:
            sent, weight = sent
            sent, summed = tie(sent, summed)
        got = exchange(sent, GROUP)
        if step == 0:
            summed = summed + swap(summed, "zh")
            got, summed = tie(got, summed)
        loss_rows.append(got[:, tokens, :128])
        everyone = got[:, :tokens].reshape(shards * rows, value_width)
        gradient = (
            lax.dot_general(
                rows_now, everyone, (((0,), (0,)), ((), ())), preferred_element_type=f32
            )
            * scale
        )
        master, first, second = adam_update(master, first, second, gradient)

    anchor_rows = anchor.astype(f32)
    summed = jnp.concatenate(
        [jnp.where(c_at == 0, summed, other), jnp.where(c_at == 0, other, summed)], axis=0
    )
    mean_delta = anchor_rows - summed / replicas
    new_moment = NESTEROV * momentum.astype(f32) + mean_delta
    global_fragment = anchor_rows - OUTER_RATE * (mean_delta + NESTEROV * new_moment)
    merged = (
        MIXING * lax.dynamic_slice(master, (zero, start), (shard_rows, frag_width))
        + (1.0 - MIXING) * global_fragment
    )
    master = lax.dynamic_update_slice(master, merged, (zero, start))
    losses = jnp.sum(jnp.stack(loss_rows).astype(f32), axis=(1, 2))
    return (master[None], losses[None])


def solution(mesh):
    fine = Mesh(mesh.devices.reshape(2, 8, 2, 4, 2, 2), REPLICA + FSDP)
    placed = (
        P(REPLICA, None, FSDP, None),
        P(REPLICA, None, FSDP, None),
        P(REPLICA, None, FSDP),
        P(REPLICA, FSDP, None),
        P(REPLICA, FSDP, None),
        P(REPLICA, FSDP, None),
        P(FSDP, None),
        P(FSDP, None),
        P(),
    )
    return jax.shard_map(
        body,
        mesh=fine,
        in_specs=placed,
        out_specs=(P(REPLICA, FSDP, None), P(REPLICA, None)),
        check_vma=False,
    )
```

```python
import functools

import jax
import jax.numpy as jnp
from jax import lax
from jax.experimental import pallas as pl
from jax.experimental.pallas import tpu as pltpu
from jax.sharding import Mesh, PartitionSpec as P

DOCS = 8


NORM_EPS = 1e-05
ADAM_EPS = 1e-08
INNER_RATE = 0.1
DECAY_RATE = 0.1
BETA_FIRST = 0.9
BETA_SECOND = 0.95
OUTER_RATE = 0.7
NESTEROV = 0.9
MIXING = 0.5

REPLICA = ("zh", "y", "c")
FSDP = ("x", "zf", "zn")
ORDER = ("x", "zn", "zf")
GROUP = ("x", "zn")
EXTRA = 16
CHUNK = 32
VMEM = 48 * 1024 * 1024
ALL_VMEM = 60 * 1024 * 1024

bf16, f32 = jnp.bfloat16, jnp.float32


def adam_update(master, first, second, gradient):
    first = BETA_FIRST * first + (1.0 - BETA_FIRST) * gradient
    second = BETA_SECOND * second + (1.0 - BETA_SECOND) * gradient * gradient
    master = master - INNER_RATE * (first / (jnp.sqrt(second) + ADAM_EPS) + DECAY_RATE * master)
    return (master, first, second)


def exchange(blocks, axes):
    return lax.all_to_all(blocks, axes, split_axis=0, concat_axis=0, tiled=False)


def swap(block, axis, bit=1):
    size = lax.axis_size(axis)
    return lax.ppermute(block, axis, [(i, i ^ bit) for i in range(size)])


def tie(*values):
    return lax.optimization_barrier(values)


def normalize_kernel(width, hidden_ref, out_ref, held, normed, arrived, sent):
    steps, rows, _ = held.shape
    parts = rows // CHUNK

    def place(at):
        return at // parts, pl.ds(pl.multiple_of((at % parts) * CHUNK, CHUNK), CHUNK)

    def take(at):
        step, here = place(at)
        return pltpu.make_async_copy(hidden_ref.at[0, step, here], held.at[step, here], arrived.at[at])

    def give(at):
        step, here = place(at)
        return pltpu.make_async_copy(
            normed.at[:, step, here], out_ref.at[:, step, here], sent.at[at]
        )

    for at in range(steps * parts):
        take(at).start()

    def chunk(at, carry):
        take(at).wait()
        step, here = place(at)
        wide = held[step, here].astype(f32)
        power = jnp.mean(wide * wide, axis=-1, keepdims=True)
        narrow = (wide * lax.rsqrt(power + NORM_EPS)).astype(bf16)
        for block in range(out_ref.shape[0]):
            x, zn, zf = block // 4, (block // 2) % 2, block % 2
            owner = x * 4 + zf * 2 + zn
            normed[block, step, here] = narrow[:, owner * width : (owner + 1) * width]
        give(at).start()
        return carry

    lax.fori_loop(0, steps * parts, chunk, 0)
    for at in range(steps * parts):
        give(at).wait()


def normalize(hidden, shards):
    _, steps, rows, model_width = hidden.shape
    width = model_width // shards
    parts = steps * rows // CHUNK
    return pl.pallas_call(
        functools.partial(normalize_kernel, width),
        in_specs=[pl.BlockSpec(memory_space=pl.ANY)],
        out_specs=pl.BlockSpec(memory_space=pl.ANY),
        out_shape=jax.ShapeDtypeStruct((shards, steps, rows, width), bf16),
        scratch_shapes=[
            pltpu.VMEM((steps, rows, model_width), bf16),
            pltpu.VMEM((shards, steps, rows, width), bf16),
            pltpu.SemaphoreType.DMA((parts,)),
            pltpu.SemaphoreType.DMA((parts,)),
        ],
        compiler_params=pltpu.CompilerParams(vmem_limit_bytes=ALL_VMEM),
        name="normalize",
    )(hidden)


def error_kernel(scale, counted, own_ref, got_ref, *rest):
    tokens, columns = 128, own_ref.shape[1]
    total = own_ref[...] + got_ref[...].astype(f32)
    if counted:
        out_ref, later_ref = rest
        counts = total[tokens : tokens + 1, :128]
        inverse = jnp.where(counts > 0.0, 1.0 / (DOCS * jnp.maximum(counts, 1.0)), 0.0)
        lane = lax.broadcasted_iota(jnp.int32, (tokens, 128), 1)
        here = lane == lax.broadcasted_iota(jnp.int32, (tokens, 128), 0)
        weights = []
        for step in range(2):
            ids = jnp.where(here, total[tokens + 1 + step : tokens + 2 + step, :128], 0.0)
            ids = jnp.sum(ids, axis=-1, keepdims=True).astype(jnp.int32) + DOCS * step
            hot = jnp.where(lane == ids, inverse, 0.0)
            weights.append(jnp.sum(hot, axis=-1, keepdims=True))
        weight = weights[0]
        later_ref[...] = jnp.broadcast_to(weights[1], later_ref.shape)
    else:
        weight_ref, out_ref = rest
        weight = weight_ref[:, :1]
    error = total[:tokens] * scale
    grad = (weight * error / columns).astype(bf16)
    each = jnp.sum(error * error, axis=-1, keepdims=True) / columns
    loss = jnp.sum(weight * 0.5 * each, axis=0, keepdims=True)
    high = loss.astype(bf16).astype(f32)
    middle = (loss - high).astype(bf16).astype(f32)
    low = loss - high - middle
    lane = lax.broadcasted_iota(jnp.int32, (EXTRA, columns), 1)
    lane = lane + columns * lax.broadcasted_iota(jnp.int32, (EXTRA, columns), 0)
    row = jnp.where(lane == 0, high, jnp.where(lane == 1, middle, jnp.where(lane == 2, low, 0.0)))
    row = row.astype(bf16)
    for at in range(out_ref.shape[0]):
        out_ref[at, :tokens] = grad
        out_ref[at, tokens:] = row


def errors(own, got, weight, tokens, copies, scale):
    columns = own.shape[1]
    sent = jax.ShapeDtypeStruct((copies, tokens + EXTRA, columns), bf16)
    kept = jax.ShapeDtypeStruct((tokens, 128), f32)
    counted = weight is None
    return pl.pallas_call(
        functools.partial(error_kernel, scale, counted),
        out_shape=(sent, kept) if counted else sent,
        compiler_params=pltpu.CompilerParams(vmem_limit_bytes=VMEM),
        cost_estimate=pl.CostEstimate(
            flops=8 * tokens * columns, bytes_accessed=30 * tokens * columns, transcendentals=0
        ),
        name="errors",
    )(own, got, *(() if counted else (weight,)))


def project_kernel(columns_ref, weights_ref, counts_ref, out_ref, first_ref, later_ref, made, sent):
    shards, _, rows, _ = columns_ref.shape
    groups, tokens, _ = made.shape
    tokens = tokens - EXTRA
    share = tokens // rows

    def give(at):
        return pltpu.make_async_copy(made.at[pl.ds(at, 2)], out_ref.at[pl.ds(at, 2)], sent.at[at // 2])

    for at in range(0, groups, 2):
        for shard in range(at * share, (at + 2) * share):
            first_ref[shard * rows : (shard + 1) * rows] = columns_ref[shard, 0]
        product = jnp.dot(
            first_ref[at * tokens : (at + 2) * tokens], weights_ref[0], preferred_element_type=f32
        ).astype(bf16)
        for group in range(2):
            made[at + group, :tokens] = product[group * tokens : (group + 1) * tokens]
            made[at + group, tokens:] = counts_ref[...]
        give(at).start()
    for shard in range(shards):
        later_ref[shard * rows : (shard + 1) * rows] = columns_ref[shard, 1]
    for at in range(0, groups, 2):
        give(at).wait()


def project(columns, weights, count_rows, groups):
    shards, _, rows, features = columns.shape
    tokens, wide = shards * rows, weights.shape[2]
    block = jax.ShapeDtypeStruct((groups, tokens // groups + EXTRA, wide), bf16)
    plain = jax.ShapeDtypeStruct((tokens, features), bf16)
    vmem = pl.BlockSpec(memory_space=pltpu.MemorySpace.VMEM)
    return pl.pallas_call(
        project_kernel,
        in_specs=[vmem, vmem, vmem],
        out_specs=(pl.BlockSpec(memory_space=pl.ANY), vmem, vmem),
        out_shape=(block, plain, plain),
        scratch_shapes=[pltpu.VMEM(block.shape, bf16), pltpu.SemaphoreType.DMA((groups // 2,))],
        compiler_params=pltpu.CompilerParams(vmem_limit_bytes=VMEM),
        name="project",
    )(columns, weights, count_rows)


def body(hidden, targets, doc_ids, weights, adam_m, adam_v, anchor, momentum, fragment):
    steps_total, rows, model_width = hidden.shape[1:]
    shard_rows, value_width = weights.shape[1:]
    frag_width = anchor.shape[1]
    nx, nn, nf = (lax.axis_size(a) for a in ORDER)
    shards, groups = nx * nn * nf, nx * nn
    f_at, c_at = lax.axis_index("zf"), lax.axis_index("c")
    scale = model_width ** (-0.5)
    zero = jnp.zeros((), jnp.int32)
    start = fragment[0] * frag_width
    replicas = lax.axis_size(REPLICA)
    tokens = nf * rows

    def pick(array, at, axis):
        return lax.dynamic_index_in_dim(array, at, axis, keepdims=False)

    blocks = normalize(hidden, shards)
    blocks, weights, targets, doc_ids = tie(blocks, weights, targets, doc_ids)
    columns = exchange(blocks, ORDER)

    doc_range = jnp.arange(DOCS, dtype=jnp.int32)
    counts = jnp.sum((doc_ids[0][..., None] == doc_range).astype(f32), axis=1)
    count_rows = jnp.pad(
        counts.reshape(1, -1).astype(bf16),
        ((0, EXTRA - 1), (0, value_width - steps_total * DOCS)),
    )
    goal = targets[0].astype(f32) / scale
    goal = jnp.concatenate([jnp.where(f_at == at, goal, 0.0) for at in range(nf)], axis=1)
    ids = doc_ids[0].astype(f32)
    ids = jnp.concatenate([jnp.where(f_at == at, ids, 0.0) for at in range(nf)], axis=1)
    ids = jnp.pad(ids, ((1, EXTRA - 1 - steps_total), (0, value_width - tokens)))
    goal = [jnp.concatenate([goal[0], -ids], axis=0), goal[1]]

    half = shard_rows // 2
    local = lax.dynamic_slice(weights[0], (zero, start), (shard_rows, frag_width))
    local = local.reshape(2, half, frag_width)
    summed = pick(local, c_at, 0).astype(f32) + swap(pick(local, c_at ^ 1, 0), "c").astype(f32)
    for axis, bit in (("y", 1), ("y", 2), ("zh", 1)):
        summed = summed + swap(summed, axis, bit)

    columns, goal, count_rows, summed = tie(columns, goal, count_rows, summed)
    partial, *step_rows = project(columns, weights, count_rows, groups)

    master = weights[0].astype(f32)
    first = adam_m[0].astype(f32)
    second = adam_v[0].astype(f32)
    loss_rows, weight = [], None
    for step in range(steps_total):
        rows_now = step_rows[step]
        if step == 1:
            partial = jnp.dot(rows_now, master.astype(bf16), preferred_element_type=f32)
            partial = partial.astype(bf16).reshape(groups, tokens, value_width)
            partial, summed = tie(partial, summed)
        partial = exchange(partial, GROUP)
        if step == 1:
            other = swap(summed, "c")
            partial, summed, other = tie(partial, summed, other)
        own = jnp.sum(partial.astype(f32), axis=0) - goal[step]
        got = swap(own.astype(bf16), "zf")
        sent = errors(own, got, weight, tokens, groups, scale)
        if step == 0:
            sent, weight = sent
            sent, summed = tie(sent, summed)
        got = exchange(sent, GROUP)
        if step == 0:
            summed = summed + swap(summed, "y", 4)
            got, summed = tie(got, summed)
        loss_rows.append(got[:, tokens, :128])
        everyone = got[:, :tokens].reshape(shards * rows, value_width)
        gradient = (
            lax.dot_general(
                rows_now, everyone, (((0,), (0,)), ((), ())), preferred_element_type=f32
            )
            * scale
        )
        master, first, second = adam_update(master, first, second, gradient)

    anchor_rows = anchor.astype(f32)
    summed = jnp.concatenate(
        [jnp.where(c_at == 0, summed, other), jnp.where(c_at == 0, other, summed)], axis=0
    )
    mean_delta = anchor_rows - summed / replicas
    new_moment = NESTEROV * momentum.astype(f32) + mean_delta
    global_fragment = anchor_rows - OUTER_RATE * (mean_delta + NESTEROV * new_moment)
    merged = (
        MIXING * lax.dynamic_slice(master, (zero, start), (shard_rows, frag_width))
        + (1.0 - MIXING) * global_fragment
    )
    master = lax.dynamic_update_slice(master, merged, (zero, start))
    losses = jnp.sum(jnp.stack(loss_rows).astype(f32), axis=(1, 2))
    return (master[None], losses[None])


def solution(mesh):
    fine = Mesh(mesh.devices.reshape(2, 8, 2, 4, 2, 2), REPLICA + FSDP)
    placed = (
        P(REPLICA, None, FSDP, None),
        P(REPLICA, None, FSDP, None),
        P(REPLICA, None, FSDP),
        P(REPLICA, FSDP, None),
        P(REPLICA, FSDP, None),
        P(REPLICA, FSDP, None),
        P(FSDP, None),
        P(FSDP, None),
        P(),
    )
    return jax.shard_map(
        body,
        mesh=fine,
        in_specs=placed,
        out_specs=(P(REPLICA, FSDP, None), P(REPLICA, None)),
        check_vma=False,
    )
```

```python
import functools

import jax
import jax.numpy as jnp
from jax import lax
from jax.experimental import pallas as pl
from jax.experimental.pallas import tpu as pltpu
from jax.sharding import Mesh, PartitionSpec as P

DOCS = 8


NORM_EPS = 1e-05
ADAM_EPS = 1e-08
INNER_RATE = 0.1
DECAY_RATE = 0.1
BETA_FIRST = 0.9
BETA_SECOND = 0.95
OUTER_RATE = 0.7
NESTEROV = 0.9
MIXING = 0.5

REPLICA = ("zh", "y", "c")
FSDP = ("x", "zf", "zn")
ORDER = ("x", "zn", "zf")
GROUP = ("x", "zn")
EXTRA = 16
CHUNK = 32
VMEM = 48 * 1024 * 1024
ALL_VMEM = 60 * 1024 * 1024

bf16, f32 = jnp.bfloat16, jnp.float32


def adam_update(master, first, second, gradient):
    first = BETA_FIRST * first + (1.0 - BETA_FIRST) * gradient
    second = BETA_SECOND * second + (1.0 - BETA_SECOND) * gradient * gradient
    master = master - INNER_RATE * (first / (jnp.sqrt(second) + ADAM_EPS) + DECAY_RATE * master)
    return (master, first, second)


def exchange(blocks, axes):
    return lax.all_to_all(blocks, axes, split_axis=0, concat_axis=0, tiled=False)


def swap(block, axis, bit=1):
    size = lax.axis_size(axis)
    return lax.ppermute(block, axis, [(i, i ^ bit) for i in range(size)])


def tie(*values):
    return lax.optimization_barrier(values)


def normalize_kernel(width, hidden_ref, out_ref, held, normed, arrived, sent):
    steps, rows, _ = held.shape
    parts = rows // CHUNK

    def place(at):
        return at // parts, pl.ds(pl.multiple_of((at % parts) * CHUNK, CHUNK), CHUNK)

    def take(at):
        step, here = place(at)
        return pltpu.make_async_copy(hidden_ref.at[0, step, here], held.at[step, here], arrived.at[at])

    def give(at):
        step, here = place(at)
        return pltpu.make_async_copy(
            normed.at[:, step, here], out_ref.at[:, step, here], sent.at[at]
        )

    for at in range(steps * parts):
        take(at).start()

    def chunk(at, carry):
        take(at).wait()
        step, here = place(at)
        wide = held[step, here].astype(f32)
        power = jnp.mean(wide * wide, axis=-1, keepdims=True)
        narrow = (wide * lax.rsqrt(power + NORM_EPS)).astype(bf16)
        for block in range(out_ref.shape[0]):
            x, zn, zf = block // 4, (block // 2) % 2, block % 2
            owner = x * 4 + zf * 2 + zn
            normed[block, step, here] = narrow[:, owner * width : (owner + 1) * width]
        give(at).start()
        return carry

    lax.fori_loop(0, steps * parts, chunk, 0)
    for at in range(steps * parts):
        give(at).wait()


def normalize(hidden, shards):
    _, steps, rows, model_width = hidden.shape
    width = model_width // shards
    parts = steps * rows // CHUNK
    return pl.pallas_call(
        functools.partial(normalize_kernel, width),
        in_specs=[pl.BlockSpec(memory_space=pl.ANY)],
        out_specs=pl.BlockSpec(memory_space=pl.ANY),
        out_shape=jax.ShapeDtypeStruct((shards, steps, rows, width), bf16),
        scratch_shapes=[
            pltpu.VMEM((steps, rows, model_width), bf16),
            pltpu.VMEM((shards, steps, rows, width), bf16),
            pltpu.SemaphoreType.DMA((parts,)),
            pltpu.SemaphoreType.DMA((parts,)),
        ],
        compiler_params=pltpu.CompilerParams(vmem_limit_bytes=ALL_VMEM),
        name="normalize",
    )(hidden)


def error_kernel(scale, counted, own_ref, got_ref, *rest):
    tokens, columns = 128, own_ref.shape[1]
    total = own_ref[...] + got_ref[...].astype(f32)
    if counted:
        out_ref, later_ref = rest
        counts = total[tokens : tokens + 1, :128]
        inverse = jnp.where(counts > 0.0, 1.0 / (DOCS * jnp.maximum(counts, 1.0)), 0.0)
        lane = lax.broadcasted_iota(jnp.int32, (tokens, 128), 1)
        here = lane == lax.broadcasted_iota(jnp.int32, (tokens, 128), 0)
        weights = []
        for step in range(2):
            ids = jnp.where(here, total[tokens + 1 + step : tokens + 2 + step, :128], 0.0)
            ids = jnp.sum(ids, axis=-1, keepdims=True).astype(jnp.int32) + DOCS * step
            hot = jnp.where(lane == ids, inverse, 0.0)
            weights.append(jnp.sum(hot, axis=-1, keepdims=True))
        weight = weights[0]
        later_ref[...] = jnp.broadcast_to(weights[1], later_ref.shape)
    else:
        weight_ref, out_ref = rest
        weight = weight_ref[:, :1]
    error = total[:tokens] * scale
    grad = (weight * error / columns).astype(bf16)
    each = jnp.sum(error * error, axis=-1, keepdims=True) / columns
    loss = jnp.sum(weight * 0.5 * each, axis=0, keepdims=True)
    high = loss.astype(bf16).astype(f32)
    middle = (loss - high).astype(bf16).astype(f32)
    low = loss - high - middle
    lane = lax.broadcasted_iota(jnp.int32, (EXTRA, columns), 1)
    lane = lane + columns * lax.broadcasted_iota(jnp.int32, (EXTRA, columns), 0)
    row = jnp.where(lane == 0, high, jnp.where(lane == 1, middle, jnp.where(lane == 2, low, 0.0)))
    row = row.astype(bf16)
    for at in range(out_ref.shape[0]):
        out_ref[at, :tokens] = grad
        out_ref[at, tokens:] = row


def errors(own, got, weight, tokens, copies, scale):
    columns = own.shape[1]
    sent = jax.ShapeDtypeStruct((copies, tokens + EXTRA, columns), bf16)
    kept = jax.ShapeDtypeStruct((tokens, 128), f32)
    counted = weight is None
    return pl.pallas_call(
        functools.partial(error_kernel, scale, counted),
        out_shape=(sent, kept) if counted else sent,
        compiler_params=pltpu.CompilerParams(vmem_limit_bytes=VMEM),
        cost_estimate=pl.CostEstimate(
            flops=8 * tokens * columns, bytes_accessed=30 * tokens * columns, transcendentals=0
        ),
        name="errors",
    )(own, got, *(() if counted else (weight,)))


def project_kernel(columns_ref, weights_ref, counts_ref, out_ref, first_ref, later_ref, made, sent):
    shards, _, rows, _ = columns_ref.shape
    groups, tokens, _ = made.shape
    tokens = tokens - EXTRA
    share = tokens // rows

    def give(at):
        return pltpu.make_async_copy(made.at[pl.ds(at, 2)], out_ref.at[pl.ds(at, 2)], sent.at[at // 2])

    for at in range(0, groups, 2):
        for shard in range(at * share, (at + 2) * share):
            first_ref[shard * rows : (shard + 1) * rows] = columns_ref[shard, 0]
        product = jnp.dot(
            first_ref[at * tokens : (at + 2) * tokens], weights_ref[0], preferred_element_type=f32
        ).astype(bf16)
        for group in range(2):
            made[at + group, :tokens] = product[group * tokens : (group + 1) * tokens]
            made[at + group, tokens:] = counts_ref[...]
        give(at).start()
    for shard in range(shards):
        later_ref[shard * rows : (shard + 1) * rows] = columns_ref[shard, 1]
    for at in range(0, groups, 2):
        give(at).wait()


def project(columns, weights, count_rows, groups):
    shards, _, rows, features = columns.shape
    tokens, wide = shards * rows, weights.shape[2]
    block = jax.ShapeDtypeStruct((groups, tokens // groups + EXTRA, wide), bf16)
    plain = jax.ShapeDtypeStruct((tokens, features), bf16)
    vmem = pl.BlockSpec(memory_space=pltpu.MemorySpace.VMEM)
    return pl.pallas_call(
        project_kernel,
        in_specs=[vmem, vmem, vmem],
        out_specs=(pl.BlockSpec(memory_space=pl.ANY), vmem, vmem),
        out_shape=(block, plain, plain),
        scratch_shapes=[pltpu.VMEM(block.shape, bf16), pltpu.SemaphoreType.DMA((groups // 2,))],
        compiler_params=pltpu.CompilerParams(vmem_limit_bytes=VMEM),
        name="project",
    )(columns, weights, count_rows)


def body(hidden, targets, doc_ids, weights, adam_m, adam_v, anchor, momentum, fragment):
    steps_total, rows, model_width = hidden.shape[1:]
    shard_rows, value_width = weights.shape[1:]
    frag_width = anchor.shape[1]
    nx, nn, nf = (lax.axis_size(a) for a in ORDER)
    shards, groups = nx * nn * nf, nx * nn
    f_at, c_at = lax.axis_index("zf"), lax.axis_index("c")
    scale = model_width ** (-0.5)
    zero = jnp.zeros((), jnp.int32)
    start = fragment[0] * frag_width
    replicas = lax.axis_size(REPLICA)
    tokens = nf * rows

    def pick(array, at, axis):
        return lax.dynamic_index_in_dim(array, at, axis, keepdims=False)

    blocks = normalize(hidden, shards)
    blocks, weights, targets, doc_ids = tie(blocks, weights, targets, doc_ids)
    columns = exchange(blocks, ORDER)

    doc_range = jnp.arange(DOCS, dtype=jnp.int32)
    counts = jnp.sum((doc_ids[0][..., None] == doc_range).astype(f32), axis=1)
    count_rows = jnp.pad(
        counts.reshape(1, -1).astype(bf16),
        ((0, EXTRA - 1), (0, value_width - steps_total * DOCS)),
    )
    goal = targets[0].astype(f32) / scale
    goal = jnp.concatenate([jnp.where(f_at == at, goal, 0.0) for at in range(nf)], axis=1)
    ids = doc_ids[0].astype(f32)
    ids = jnp.concatenate([jnp.where(f_at == at, ids, 0.0) for at in range(nf)], axis=1)
    ids = jnp.pad(ids, ((1, EXTRA - 1 - steps_total), (0, value_width - tokens)))
    goal = [jnp.concatenate([goal[0], -ids], axis=0), goal[1]]

    half = shard_rows // 2
    local = lax.dynamic_slice(weights[0], (zero, start), (shard_rows, frag_width))
    local = local.reshape(2, half, frag_width)
    summed = pick(local, c_at, 0).astype(f32) + swap(pick(local, c_at ^ 1, 0), "c").astype(f32)
    y_at = lax.rem(lax.axis_index("y"), 2)
    summed = summed.reshape(2, half // 2, frag_width)
    summed = pick(summed, y_at, 0) + swap(pick(summed, y_at ^ 1, 0), "y")
    for axis, bit in (("y", 2), ("zh", 1)):
        summed = summed + swap(summed, axis, bit)

    def whole(mine, other, at):
        return jnp.concatenate([jnp.where(at == 0, mine, other), jnp.where(at == 0, other, mine)])

    columns, goal, count_rows, summed = tie(columns, goal, count_rows, summed)
    partial, *step_rows = project(columns, weights, count_rows, groups)

    master = weights[0].astype(f32)
    first = adam_m[0].astype(f32)
    second = adam_v[0].astype(f32)
    anchor_rows = anchor.astype(f32)
    loss_rows, weight = [], None
    for step in range(steps_total):
        rows_now = step_rows[step]
        if step == 1:
            partial = jnp.dot(rows_now, master.astype(bf16), preferred_element_type=f32)
            partial = partial.astype(bf16).reshape(groups, tokens, value_width)
            partial, summed = tie(partial, summed)
        partial = exchange(partial, GROUP)
        if step == 1:
            summed = whole(summed, swap(summed, "y"), y_at)
            partial, summed = tie(partial, summed)
        own = jnp.sum(partial.astype(f32), axis=0) - goal[step]
        got = swap(own.astype(bf16), "zf")
        sent = errors(own, got, weight, tokens, groups, scale)
        if step == 0:
            sent, weight = sent
        sent, summed = tie(sent, summed)
        got = exchange(sent, GROUP)
        if step == 0:
            summed = summed + swap(summed, "y", 4)
            got, summed = tie(got, summed)
        else:
            summed = whole(summed, swap(summed, "c"), c_at)
            mean_delta = anchor_rows - summed / replicas
            new_moment = NESTEROV * momentum.astype(f32) + mean_delta
            global_fragment = anchor_rows - OUTER_RATE * (mean_delta + NESTEROV * new_moment)
            got, global_fragment = tie(got, global_fragment)
        loss_rows.append(got[:, tokens, :128])
        everyone = got[:, :tokens].reshape(shards * rows, value_width)
        gradient = (
            lax.dot_general(
                rows_now, everyone, (((0,), (0,)), ((), ())), preferred_element_type=f32
            )
            * scale
        )
        master, first, second = adam_update(master, first, second, gradient)

    merged = (
        MIXING * lax.dynamic_slice(master, (zero, start), (shard_rows, frag_width))
        + (1.0 - MIXING) * global_fragment
    )
    master = lax.dynamic_update_slice(master, merged, (zero, start))
    losses = jnp.sum(jnp.stack(loss_rows).astype(f32), axis=(1, 2))
    return (master[None], losses[None])


def solution(mesh):
    fine = Mesh(mesh.devices.reshape(2, 8, 2, 4, 2, 2), REPLICA + FSDP)
    placed = (
        P(REPLICA, None, FSDP, None),
        P(REPLICA, None, FSDP, None),
        P(REPLICA, None, FSDP),
        P(REPLICA, FSDP, None),
        P(REPLICA, FSDP, None),
        P(REPLICA, FSDP, None),
        P(FSDP, None),
        P(FSDP, None),
        P(),
    )
    return jax.shard_map(
        body,
        mesh=fine,
        in_specs=placed,
        out_specs=(P(REPLICA, FSDP, None), P(REPLICA, None)),
        check_vma=False,
    )
```

```python
import functools

import jax
import jax.numpy as jnp
from jax import lax
from jax.experimental import pallas as pl
from jax.experimental.pallas import tpu as pltpu
from jax.sharding import Mesh, PartitionSpec as P

DOCS = 8


NORM_EPS = 1e-05
ADAM_EPS = 1e-08
INNER_RATE = 0.1
DECAY_RATE = 0.1
BETA_FIRST = 0.9
BETA_SECOND = 0.95
OUTER_RATE = 0.7
NESTEROV = 0.9
MIXING = 0.5

REPLICA = ("zh", "y", "c")
FSDP = ("x", "zf", "zn")
ORDER = ("x", "zn", "zf")
GROUP = ("x", "zn")
EXTRA = 16
CHUNK = 32
VMEM = 48 * 1024 * 1024
ALL_VMEM = 60 * 1024 * 1024

bf16, f32 = jnp.bfloat16, jnp.float32


def adam_update(master, first, second, gradient):
    first = BETA_FIRST * first + (1.0 - BETA_FIRST) * gradient
    second = BETA_SECOND * second + (1.0 - BETA_SECOND) * gradient * gradient
    master = master - INNER_RATE * (first / (jnp.sqrt(second) + ADAM_EPS) + DECAY_RATE * master)
    return (master, first, second)


def exchange(blocks, axes):
    return lax.all_to_all(blocks, axes, split_axis=0, concat_axis=0, tiled=False)


def swap(block, axis, bit=1):
    size = lax.axis_size(axis)
    return lax.ppermute(block, axis, [(i, i ^ bit) for i in range(size)])


def tie(*values):
    return lax.optimization_barrier(values)


def normalize_kernel(width, hidden_ref, out_ref, held, normed, arrived, sent):
    steps, rows, _ = held.shape
    parts = rows // CHUNK

    def place(at):
        return at // parts, pl.ds(pl.multiple_of((at % parts) * CHUNK, CHUNK), CHUNK)

    def take(at):
        step, here = place(at)
        return pltpu.make_async_copy(hidden_ref.at[0, step, here], held.at[step, here], arrived.at[at])

    def give(at):
        step, here = place(at)
        return pltpu.make_async_copy(
            normed.at[:, step, here], out_ref.at[:, step, here], sent.at[at]
        )

    for at in range(steps * parts):
        take(at).start()

    def chunk(at, carry):
        take(at).wait()
        step, here = place(at)
        wide = held[step, here].astype(f32)
        power = jnp.mean(wide * wide, axis=-1, keepdims=True)
        narrow = (wide * lax.rsqrt(power + NORM_EPS)).astype(bf16)
        for block in range(out_ref.shape[0]):
            x, zn, zf = block // 4, (block // 2) % 2, block % 2
            owner = x * 4 + zf * 2 + zn
            normed[block, step, here] = narrow[:, owner * width : (owner + 1) * width]
        give(at).start()
        return carry

    lax.fori_loop(0, steps * parts, chunk, 0)
    for at in range(steps * parts):
        give(at).wait()


def normalize(hidden, shards):
    _, steps, rows, model_width = hidden.shape
    width = model_width // shards
    parts = steps * rows // CHUNK
    return pl.pallas_call(
        functools.partial(normalize_kernel, width),
        in_specs=[pl.BlockSpec(memory_space=pl.ANY)],
        out_specs=pl.BlockSpec(memory_space=pl.ANY),
        out_shape=jax.ShapeDtypeStruct((shards, steps, rows, width), bf16),
        scratch_shapes=[
            pltpu.VMEM((steps, rows, model_width), bf16),
            pltpu.VMEM((shards, steps, rows, width), bf16),
            pltpu.SemaphoreType.DMA((parts,)),
            pltpu.SemaphoreType.DMA((parts,)),
        ],
        compiler_params=pltpu.CompilerParams(vmem_limit_bytes=ALL_VMEM),
        name="normalize",
    )(hidden)


def error_kernel(scale, counted, own_ref, got_ref, *rest):
    tokens, columns = 128, own_ref.shape[1]
    total = own_ref[...] + got_ref[...].astype(f32)
    if counted:
        out_ref, later_ref = rest
        counts = total[tokens : tokens + 1, :128]
        inverse = jnp.where(counts > 0.0, 1.0 / (DOCS * jnp.maximum(counts, 1.0)), 0.0)
        lane = lax.broadcasted_iota(jnp.int32, (tokens, 128), 1)
        here = lane == lax.broadcasted_iota(jnp.int32, (tokens, 128), 0)
        weights = []
        for step in range(2):
            ids = jnp.where(here, total[tokens + 1 + step : tokens + 2 + step, :128], 0.0)
            ids = jnp.sum(ids, axis=-1, keepdims=True).astype(jnp.int32) + DOCS * step
            hot = jnp.where(lane == ids, inverse, 0.0)
            weights.append(jnp.sum(hot, axis=-1, keepdims=True))
        weight = weights[0]
        later_ref[...] = jnp.broadcast_to(weights[1], later_ref.shape)
    else:
        weight_ref, out_ref = rest
        weight = weight_ref[:, :1]
    error = total[:tokens] * scale
    grad = (weight * error / columns).astype(bf16)
    each = jnp.sum(error * error, axis=-1, keepdims=True) / columns
    loss = jnp.sum(weight * 0.5 * each, axis=0, keepdims=True)
    high = loss.astype(bf16).astype(f32)
    middle = (loss - high).astype(bf16).astype(f32)
    low = loss - high - middle
    lane = lax.broadcasted_iota(jnp.int32, (EXTRA, columns), 1)
    lane = lane + columns * lax.broadcasted_iota(jnp.int32, (EXTRA, columns), 0)
    row = jnp.where(lane == 0, high, jnp.where(lane == 1, middle, jnp.where(lane == 2, low, 0.0)))
    row = row.astype(bf16)
    for at in range(out_ref.shape[0]):
        out_ref[at, :tokens] = grad
        out_ref[at, tokens:] = row


def errors(own, got, weight, tokens, copies, scale):
    columns = own.shape[1]
    sent = jax.ShapeDtypeStruct((copies, tokens + EXTRA, columns), bf16)
    kept = jax.ShapeDtypeStruct((tokens, 128), f32)
    counted = weight is None
    return pl.pallas_call(
        functools.partial(error_kernel, scale, counted),
        out_shape=(sent, kept) if counted else sent,
        compiler_params=pltpu.CompilerParams(vmem_limit_bytes=VMEM),
        cost_estimate=pl.CostEstimate(
            flops=8 * tokens * columns, bytes_accessed=30 * tokens * columns, transcendentals=0
        ),
        name="errors",
    )(own, got, *(() if counted else (weight,)))


def project_kernel(columns_ref, weights_ref, counts_ref, out_ref, first_ref, made, sent):
    shards, _, rows, _ = columns_ref.shape
    groups, tokens, _ = made.shape
    tokens = tokens - EXTRA
    share = tokens // rows

    def give(at):
        return pltpu.make_async_copy(made.at[pl.ds(at, 2)], out_ref.at[pl.ds(at, 2)], sent.at[at // 2])

    for at in range(0, groups, 2):
        for shard in range(at * share, (at + 2) * share):
            first_ref[shard * rows : (shard + 1) * rows] = columns_ref[shard, 0]
        product = jnp.dot(
            first_ref[at * tokens : (at + 2) * tokens], weights_ref[0], preferred_element_type=f32
        ).astype(bf16)
        for group in range(2):
            made[at + group, :tokens] = product[group * tokens : (group + 1) * tokens]
            made[at + group, tokens:] = counts_ref[...]
        give(at).start()
    for at in range(0, groups, 2):
        give(at).wait()


def project(columns, weights, count_rows, groups):
    shards, _, rows, features = columns.shape
    tokens, wide = shards * rows, weights.shape[2]
    block = jax.ShapeDtypeStruct((groups, tokens // groups + EXTRA, wide), bf16)
    vmem = pl.BlockSpec(memory_space=pltpu.MemorySpace.VMEM)
    return pl.pallas_call(
        project_kernel,
        in_specs=[vmem, vmem, vmem],
        out_specs=pl.BlockSpec(memory_space=pl.ANY),
        out_shape=block,
        scratch_shapes=[
            pltpu.VMEM((tokens, features), bf16),
            pltpu.VMEM(block.shape, bf16),
            pltpu.SemaphoreType.DMA((groups // 2,)),
        ],
        compiler_params=pltpu.CompilerParams(vmem_limit_bytes=VMEM),
        name="project",
    )(columns, weights, count_rows)


def body(hidden, targets, doc_ids, weights, adam_m, adam_v, anchor, momentum, fragment):
    steps_total, rows, model_width = hidden.shape[1:]
    shard_rows, value_width = weights.shape[1:]
    frag_width = anchor.shape[1]
    nx, nn, nf = (lax.axis_size(a) for a in ORDER)
    shards, groups = nx * nn * nf, nx * nn
    f_at, c_at = lax.axis_index("zf"), lax.axis_index("c")
    scale = model_width ** (-0.5)
    zero = jnp.zeros((), jnp.int32)
    start = fragment[0] * frag_width
    replicas = lax.axis_size(REPLICA)
    tokens = nf * rows

    def pick(array, at, axis):
        return lax.dynamic_index_in_dim(array, at, axis, keepdims=False)

    blocks = normalize(hidden, shards)
    blocks, weights, targets, doc_ids = tie(blocks, weights, targets, doc_ids)
    columns = exchange(blocks, ORDER)

    doc_range = jnp.arange(DOCS, dtype=jnp.int32)
    counts = jnp.sum((doc_ids[0][..., None] == doc_range).astype(f32), axis=1)
    count_rows = jnp.pad(
        counts.reshape(1, -1).astype(bf16),
        ((0, EXTRA - 1), (0, value_width - steps_total * DOCS)),
    )
    goal = targets[0].astype(f32) / scale
    goal = jnp.concatenate([jnp.where(f_at == at, goal, 0.0) for at in range(nf)], axis=1)
    ids = doc_ids[0].astype(f32)
    ids = jnp.concatenate([jnp.where(f_at == at, ids, 0.0) for at in range(nf)], axis=1)
    ids = jnp.pad(ids, ((1, EXTRA - 1 - steps_total), (0, value_width - tokens)))
    goal = [jnp.concatenate([goal[0], -ids], axis=0), goal[1]]

    half = shard_rows // 2
    local = lax.dynamic_slice(weights[0], (zero, start), (shard_rows, frag_width))
    local = local.reshape(2, half, frag_width)
    summed = pick(local, c_at, 0).astype(f32) + swap(pick(local, c_at ^ 1, 0), "c").astype(f32)
    y_at = lax.rem(lax.axis_index("y"), 2)
    summed = summed.reshape(2, half // 2, frag_width)
    summed = pick(summed, y_at, 0) + swap(pick(summed, y_at ^ 1, 0), "y")
    for axis, bit in (("y", 2), ("zh", 1)):
        summed = summed + swap(summed, axis, bit)

    def whole(mine, other, at):
        return jnp.concatenate([jnp.where(at == 0, mine, other), jnp.where(at == 0, other, mine)])

    columns, goal, count_rows, summed = tie(columns, goal, count_rows, summed)
    partial = project(columns, weights, count_rows, groups)

    master = weights[0].astype(f32)
    first = adam_m[0].astype(f32)
    second = adam_v[0].astype(f32)
    anchor_rows = anchor.astype(f32)
    loss_rows, weight = [], None
    for step in range(steps_total):
        if step == 1:
            rows_now = step_rows[1]
            partial = jnp.dot(rows_now, master.astype(bf16), preferred_element_type=f32)
            partial = partial.astype(bf16).reshape(groups, tokens, value_width)
            partial, summed = tie(partial, summed)
        partial = exchange(partial, GROUP)
        if step == 1:
            summed = whole(summed, swap(summed, "y"), y_at)
            partial, summed = tie(partial, summed)
        own = jnp.sum(partial.astype(f32), axis=0) - goal[step]
        got = swap(own.astype(bf16), "zf")
        sent = errors(own, got, weight, tokens, groups, scale)
        if step == 0:
            sent, weight = sent
            sent, columns = tie(sent, columns)
        sent, summed = tie(sent, summed)
        got = exchange(sent, GROUP)
        if step == 0:
            summed = summed + swap(summed, "y", 4)
            step_rows = [columns[:, at].reshape(shards * rows, -1) for at in range(steps_total)]
            spaced = step_rows[0].reshape(groups, tokens, -1)
            spaced = jnp.pad(spaced, ((0, 0), (0, EXTRA), (0, 0)))
            step_rows[0] = spaced.reshape(groups * (tokens + EXTRA), -1)
            got, summed, step_rows = tie(got, summed, step_rows)
            rows_now = step_rows[0]
        else:
            summed = whole(summed, swap(summed, "c"), c_at)
            mean_delta = anchor_rows - summed / replicas
            new_moment = NESTEROV * momentum.astype(f32) + mean_delta
            global_fragment = anchor_rows - OUTER_RATE * (mean_delta + NESTEROV * new_moment)
            got, global_fragment = tie(got, global_fragment)
        loss_rows.append(got[:, tokens, :128])
        everyone = got.reshape(-1, value_width) if step == 0 else got[:, :tokens].reshape(-1, value_width)
        gradient = (
            lax.dot_general(
                rows_now, everyone, (((0,), (0,)), ((), ())), preferred_element_type=f32
            )
            * scale
        )
        master, first, second = adam_update(master, first, second, gradient)

    merged = (
        MIXING * lax.dynamic_slice(master, (zero, start), (shard_rows, frag_width))
        + (1.0 - MIXING) * global_fragment
    )
    master = lax.dynamic_update_slice(master, merged, (zero, start))
    losses = jnp.sum(jnp.stack(loss_rows).astype(f32), axis=(1, 2))
    return (master[None], losses[None])


def solution(mesh):
    fine = Mesh(mesh.devices.reshape(2, 8, 2, 4, 2, 2), REPLICA + FSDP)
    placed = (
        P(REPLICA, None, FSDP, None),
        P(REPLICA, None, FSDP, None),
        P(REPLICA, None, FSDP),
        P(REPLICA, FSDP, None),
        P(REPLICA, FSDP, None),
        P(REPLICA, FSDP, None),
        P(FSDP, None),
        P(FSDP, None),
        P(),
    )
    return jax.shard_map(
        body,
        mesh=fine,
        in_specs=placed,
        out_specs=(P(REPLICA, FSDP, None), P(REPLICA, None)),
        check_vma=False,
    )
```

```python
import functools

import jax
import jax.numpy as jnp
from jax import lax
from jax.experimental import pallas as pl
from jax.experimental.pallas import tpu as pltpu
from jax.sharding import Mesh, PartitionSpec as P

DOCS = 8


NORM_EPS = 1e-05
ADAM_EPS = 1e-08
INNER_RATE = 0.1
DECAY_RATE = 0.1
BETA_FIRST = 0.9
BETA_SECOND = 0.95
OUTER_RATE = 0.7
NESTEROV = 0.9
MIXING = 0.5

REPLICA = ("zh", "y", "c")
FSDP = ("x", "zf", "zn")
ORDER = ("x", "zn", "zf")
GROUP = ("x", "zn")
EXTRA = 16
CHUNK = 32
VMEM = 48 * 1024 * 1024
ALL_VMEM = 60 * 1024 * 1024

bf16, f32 = jnp.bfloat16, jnp.float32


def adam_update(master, first, second, gradient):
    first = BETA_FIRST * first + (1.0 - BETA_FIRST) * gradient
    second = BETA_SECOND * second + (1.0 - BETA_SECOND) * gradient * gradient
    master = master - INNER_RATE * (first / (jnp.sqrt(second) + ADAM_EPS) + DECAY_RATE * master)
    return (master, first, second)


def exchange(blocks, axes):
    return lax.all_to_all(blocks, axes, split_axis=0, concat_axis=0, tiled=False)


def swap(block, axis, bit=1):
    size = lax.axis_size(axis)
    return lax.ppermute(block, axis, [(i, i ^ bit) for i in range(size)])


def tie(*values):
    return lax.optimization_barrier(values)


def normalize_kernel(width, hidden_ref, out_ref, held, normed, arrived, sent):
    steps, rows, _ = held.shape
    parts = rows // CHUNK

    def place(at):
        return at // parts, pl.ds(pl.multiple_of((at % parts) * CHUNK, CHUNK), CHUNK)

    def take(at):
        step, here = place(at)
        return pltpu.make_async_copy(hidden_ref.at[0, step, here], held.at[step, here], arrived.at[at])

    def give(at):
        step, here = place(at)
        return pltpu.make_async_copy(
            normed.at[:, step, here], out_ref.at[:, step, here], sent.at[at]
        )

    for at in range(steps * parts):
        take(at).start()

    def chunk(at, carry):
        take(at).wait()
        step, here = place(at)
        wide = held[step, here].astype(f32)
        power = jnp.mean(wide * wide, axis=-1, keepdims=True)
        narrow = (wide * lax.rsqrt(power + NORM_EPS)).astype(bf16)
        for block in range(out_ref.shape[0]):
            x, zn, zf = block // 4, (block // 2) % 2, block % 2
            owner = x * 4 + zf * 2 + zn
            normed[block, step, here] = narrow[:, owner * width : (owner + 1) * width]
        give(at).start()
        return carry

    lax.fori_loop(0, steps * parts, chunk, 0)
    for at in range(steps * parts):
        give(at).wait()


def normalize(hidden, shards):
    _, steps, rows, model_width = hidden.shape
    width = model_width // shards
    parts = steps * rows // CHUNK
    return pl.pallas_call(
        functools.partial(normalize_kernel, width),
        in_specs=[pl.BlockSpec(memory_space=pl.ANY)],
        out_specs=pl.BlockSpec(memory_space=pl.ANY),
        out_shape=jax.ShapeDtypeStruct((shards, steps, rows, width), bf16),
        scratch_shapes=[
            pltpu.VMEM((steps, rows, model_width), bf16),
            pltpu.VMEM((shards, steps, rows, width), bf16),
            pltpu.SemaphoreType.DMA((parts,)),
            pltpu.SemaphoreType.DMA((parts,)),
        ],
        compiler_params=pltpu.CompilerParams(vmem_limit_bytes=ALL_VMEM),
        name="normalize",
    )(hidden)


def error_kernel(scale, counted, own_ref, got_ref, *rest):
    tokens, columns = 128, own_ref.shape[1]
    total = own_ref[...] + got_ref[...].astype(f32)
    if counted:
        out_ref, later_ref = rest
        counts = total[tokens : tokens + 1, :128]
        inverse = jnp.where(counts > 0.0, 1.0 / (DOCS * jnp.maximum(counts, 1.0)), 0.0)
        lane = lax.broadcasted_iota(jnp.int32, (tokens, 128), 1)
        here = lane == lax.broadcasted_iota(jnp.int32, (tokens, 128), 0)
        weights = []
        for step in range(2):
            ids = jnp.where(here, total[tokens + 1 + step : tokens + 2 + step, :128], 0.0)
            ids = jnp.sum(ids, axis=-1, keepdims=True).astype(jnp.int32) + DOCS * step
            hot = jnp.where(lane == ids, inverse, 0.0)
            weights.append(jnp.sum(hot, axis=-1, keepdims=True))
        weight = weights[0]
        later_ref[...] = jnp.broadcast_to(weights[1], later_ref.shape)
    else:
        weight_ref, out_ref = rest
        weight = weight_ref[:, :1]
    error = total[:tokens] * scale
    grad = (weight * error / columns).astype(bf16)
    each = jnp.sum(error * error, axis=-1, keepdims=True) / columns
    loss = jnp.sum(weight * 0.5 * each, axis=0, keepdims=True)
    high = loss.astype(bf16).astype(f32)
    middle = (loss - high).astype(bf16).astype(f32)
    low = loss - high - middle
    lane = lax.broadcasted_iota(jnp.int32, (EXTRA, columns), 1)
    lane = lane + columns * lax.broadcasted_iota(jnp.int32, (EXTRA, columns), 0)
    row = jnp.where(lane == 0, high, jnp.where(lane == 1, middle, jnp.where(lane == 2, low, 0.0)))
    row = row.astype(bf16)
    for at in range(out_ref.shape[0]):
        out_ref[at, :tokens] = grad
        out_ref[at, tokens:] = row


def errors(own, got, weight, tokens, copies, scale):
    columns = own.shape[1]
    sent = jax.ShapeDtypeStruct((copies, tokens + EXTRA, columns), bf16)
    kept = jax.ShapeDtypeStruct((tokens, 128), f32)
    counted = weight is None
    return pl.pallas_call(
        functools.partial(error_kernel, scale, counted),
        out_shape=(sent, kept) if counted else sent,
        compiler_params=pltpu.CompilerParams(vmem_limit_bytes=VMEM),
        cost_estimate=pl.CostEstimate(
            flops=8 * tokens * columns, bytes_accessed=30 * tokens * columns, transcendentals=0
        ),
        name="errors",
    )(own, got, *(() if counted else (weight,)))


def project_kernel(columns_ref, weights_ref, counts_ref, out_ref, first_ref, later_ref, made, sent):
    shards, _, rows, _ = columns_ref.shape
    groups, block, _ = made.shape
    tokens = block - EXTRA
    share = tokens // rows

    def give(at):
        return pltpu.make_async_copy(made.at[pl.ds(at, 2)], out_ref.at[pl.ds(at, 2)], sent.at[at // 2])

    for at in range(0, groups, 2):
        for shard in range(at * share, (at + 2) * share):
            row = shard * rows + shard // share * EXTRA
            first_ref[row : row + rows] = columns_ref[shard, 0]
        for group in (at, at + 1):
            row = group * block + tokens
            first_ref[row : row + EXTRA] = jnp.zeros((EXTRA, first_ref.shape[1]), bf16)
        product = jnp.dot(
            first_ref[at * block : (at + 2) * block], weights_ref[0], preferred_element_type=f32
        ).astype(bf16)
        for group in range(2):
            made[at + group, :tokens] = product[group * block : group * block + tokens]
            made[at + group, tokens:] = counts_ref[...]
        give(at).start()
    for shard in range(shards):
        later_ref[shard * rows : (shard + 1) * rows] = columns_ref[shard, 1]
    for at in range(0, groups, 2):
        give(at).wait()


def project(columns, weights, count_rows, groups):
    shards, _, rows, features = columns.shape
    tokens, wide = shards * rows, weights.shape[2]
    block = jax.ShapeDtypeStruct((groups, tokens // groups + EXTRA, wide), bf16)
    plain = jax.ShapeDtypeStruct((tokens, features), bf16)
    spaced = jax.ShapeDtypeStruct((tokens + groups * EXTRA, features), bf16)
    vmem = pl.BlockSpec(memory_space=pltpu.MemorySpace.VMEM)
    return pl.pallas_call(
        project_kernel,
        in_specs=[vmem, vmem, vmem],
        out_specs=(pl.BlockSpec(memory_space=pl.ANY), vmem, vmem),
        out_shape=(block, spaced, plain),
        scratch_shapes=[pltpu.VMEM(block.shape, bf16), pltpu.SemaphoreType.DMA((groups // 2,))],
        compiler_params=pltpu.CompilerParams(vmem_limit_bytes=VMEM),
        name="project",
    )(columns, weights, count_rows)


def body(hidden, targets, doc_ids, weights, adam_m, adam_v, anchor, momentum, fragment):
    steps_total, rows, model_width = hidden.shape[1:]
    shard_rows, value_width = weights.shape[1:]
    frag_width = anchor.shape[1]
    nx, nn, nf = (lax.axis_size(a) for a in ORDER)
    shards, groups = nx * nn * nf, nx * nn
    f_at, c_at = lax.axis_index("zf"), lax.axis_index("c")
    scale = model_width ** (-0.5)
    zero = jnp.zeros((), jnp.int32)
    start = fragment[0] * frag_width
    replicas = lax.axis_size(REPLICA)
    tokens = nf * rows

    def pick(array, at, axis):
        return lax.dynamic_index_in_dim(array, at, axis, keepdims=False)

    blocks = normalize(hidden, shards)
    blocks, weights, targets, doc_ids = tie(blocks, weights, targets, doc_ids)
    columns = exchange(blocks, ORDER)

    doc_range = jnp.arange(DOCS, dtype=jnp.int32)
    counts = jnp.sum((doc_ids[0][..., None] == doc_range).astype(f32), axis=1)
    count_rows = jnp.pad(
        counts.reshape(1, -1).astype(bf16),
        ((0, EXTRA - 1), (0, value_width - steps_total * DOCS)),
    )
    goal = targets[0].astype(f32) / scale
    goal = jnp.concatenate([jnp.where(f_at == at, goal, 0.0) for at in range(nf)], axis=1)
    ids = doc_ids[0].astype(f32)
    ids = jnp.concatenate([jnp.where(f_at == at, ids, 0.0) for at in range(nf)], axis=1)
    ids = jnp.pad(ids, ((1, EXTRA - 1 - steps_total), (0, value_width - tokens)))
    goal = [jnp.concatenate([goal[0], -ids], axis=0), goal[1]]

    half = shard_rows // 2
    local = lax.dynamic_slice(weights[0], (zero, start), (shard_rows, frag_width))
    local = local.reshape(2, half, frag_width)
    summed = pick(local, c_at, 0).astype(f32) + swap(pick(local, c_at ^ 1, 0), "c").astype(f32)
    y_at = lax.rem(lax.axis_index("y"), 2)
    summed = summed.reshape(2, half // 2, frag_width)
    summed = pick(summed, y_at, 0) + swap(pick(summed, y_at ^ 1, 0), "y")
    for axis, bit in (("y", 2), ("zh", 1)):
        summed = summed + swap(summed, axis, bit)

    def whole(mine, other, at):
        return jnp.concatenate([jnp.where(at == 0, mine, other), jnp.where(at == 0, other, mine)])

    columns, goal, count_rows, summed = tie(columns, goal, count_rows, summed)
    partial, *step_rows = project(columns, weights, count_rows, groups)

    master = weights[0].astype(f32)
    first = adam_m[0].astype(f32)
    second = adam_v[0].astype(f32)
    anchor_rows = anchor.astype(f32)
    loss_rows, weight = [], None
    for step in range(steps_total):
        rows_now = step_rows[step]
        if step == 1:
            partial = jnp.dot(rows_now, master.astype(bf16), preferred_element_type=f32)
            partial = partial.astype(bf16).reshape(groups, tokens, value_width)
            partial, summed = tie(partial, summed)
        partial = exchange(partial, GROUP)
        if step == 1:
            summed = whole(summed, swap(summed, "y"), y_at)
            partial, summed = tie(partial, summed)
        own = jnp.sum(partial.astype(f32), axis=0) - goal[step]
        got = swap(own.astype(bf16), "zf")
        sent = errors(own, got, weight, tokens, groups, scale)
        if step == 0:
            sent, weight = sent
        sent, summed = tie(sent, summed)
        got = exchange(sent, GROUP)
        if step == 0:
            summed = summed + swap(summed, "y", 4)
            got, summed = tie(got, summed)
        else:
            summed = whole(summed, swap(summed, "c"), c_at)
            mean_delta = anchor_rows - summed / replicas
            new_moment = NESTEROV * momentum.astype(f32) + mean_delta
            global_fragment = anchor_rows - OUTER_RATE * (mean_delta + NESTEROV * new_moment)
            got, global_fragment = tie(got, global_fragment)
        loss_rows.append(got[:, tokens, :128])
        everyone = (got if step == 0 else got[:, :tokens]).reshape(-1, value_width)
        gradient = (
            lax.dot_general(
                rows_now, everyone, (((0,), (0,)), ((), ())), preferred_element_type=f32
            )
            * scale
        )
        master, first, second = adam_update(master, first, second, gradient)

    merged = (
        MIXING * lax.dynamic_slice(master, (zero, start), (shard_rows, frag_width))
        + (1.0 - MIXING) * global_fragment
    )
    master = lax.dynamic_update_slice(master, merged, (zero, start))
    losses = jnp.sum(jnp.stack(loss_rows).astype(f32), axis=(1, 2))
    return (master[None], losses[None])


def solution(mesh):
    fine = Mesh(mesh.devices.reshape(2, 8, 2, 4, 2, 2), REPLICA + FSDP)
    placed = (
        P(REPLICA, None, FSDP, None),
        P(REPLICA, None, FSDP, None),
        P(REPLICA, None, FSDP),
        P(REPLICA, FSDP, None),
        P(REPLICA, FSDP, None),
        P(REPLICA, FSDP, None),
        P(FSDP, None),
        P(FSDP, None),
        P(),
    )
    return jax.shard_map(
        body,
        mesh=fine,
        in_specs=placed,
        out_specs=(P(REPLICA, FSDP, None), P(REPLICA, None)),
        check_vma=False,
    )
```

```python
import functools

import jax
import jax.numpy as jnp
from jax import lax
from jax.experimental import pallas as pl
from jax.experimental.pallas import tpu as pltpu
from jax.sharding import Mesh, PartitionSpec as P

DOCS = 8


NORM_EPS = 1e-05
ADAM_EPS = 1e-08
INNER_RATE = 0.1
DECAY_RATE = 0.1
BETA_FIRST = 0.9
BETA_SECOND = 0.95
OUTER_RATE = 0.7
NESTEROV = 0.9
MIXING = 0.5

REPLICA = ("zh", "y", "c")
FSDP = ("x", "zf", "zn")
ORDER = ("x", "zn", "zf")
GROUP = ("x", "zn")
EXTRA = 16
CHUNK = 32
VMEM = 48 * 1024 * 1024
ALL_VMEM = 60 * 1024 * 1024

bf16, f32 = jnp.bfloat16, jnp.float32


def adam_update(master, first, second, gradient):
    first = BETA_FIRST * first + (1.0 - BETA_FIRST) * gradient
    second = BETA_SECOND * second + (1.0 - BETA_SECOND) * gradient * gradient
    master = master - INNER_RATE * (first / (jnp.sqrt(second) + ADAM_EPS) + DECAY_RATE * master)
    return (master, first, second)


def exchange(blocks, axes):
    return lax.all_to_all(blocks, axes, split_axis=0, concat_axis=0, tiled=False)


def swap(block, axis, bit=1):
    size = lax.axis_size(axis)
    return lax.ppermute(block, axis, [(i, i ^ bit) for i in range(size)])


def tie(*values):
    return lax.optimization_barrier(values)


def normalize_kernel(width, hidden_ref, out_ref, held, normed, arrived, sent):
    steps, rows, _ = held.shape
    parts = rows // CHUNK

    def place(at):
        return at // parts, pl.ds(pl.multiple_of((at % parts) * CHUNK, CHUNK), CHUNK)

    def take(at):
        step, here = place(at)
        return pltpu.make_async_copy(hidden_ref.at[0, step, here], held.at[step, here], arrived.at[at])

    def give(at):
        step, here = place(at)
        return pltpu.make_async_copy(
            normed.at[:, step, here], out_ref.at[:, step, here], sent.at[at]
        )

    for at in range(steps * parts):
        take(at).start()

    def chunk(at, carry):
        take(at).wait()
        step, here = place(at)
        wide = held[step, here].astype(f32)
        power = jnp.mean(wide * wide, axis=-1, keepdims=True)
        narrow = (wide * lax.rsqrt(power + NORM_EPS)).astype(bf16)
        for block in range(out_ref.shape[0]):
            x, zn, zf = block // 4, (block // 2) % 2, block % 2
            owner = x * 4 + zf * 2 + zn
            normed[block, step, here] = narrow[:, owner * width : (owner + 1) * width]
        give(at).start()
        return carry

    lax.fori_loop(0, steps * parts, chunk, 0)
    for at in range(steps * parts):
        give(at).wait()


def normalize(hidden, shards):
    _, steps, rows, model_width = hidden.shape
    width = model_width // shards
    parts = steps * rows // CHUNK
    return pl.pallas_call(
        functools.partial(normalize_kernel, width),
        in_specs=[pl.BlockSpec(memory_space=pl.ANY)],
        out_specs=pl.BlockSpec(memory_space=pl.ANY),
        out_shape=jax.ShapeDtypeStruct((shards, steps, rows, width), bf16),
        scratch_shapes=[
            pltpu.VMEM((steps, rows, model_width), bf16),
            pltpu.VMEM((shards, steps, rows, width), bf16),
            pltpu.SemaphoreType.DMA((parts,)),
            pltpu.SemaphoreType.DMA((parts,)),
        ],
        compiler_params=pltpu.CompilerParams(vmem_limit_bytes=ALL_VMEM),
        name="normalize",
    )(hidden)


def error_kernel(scale, counted, own_ref, got_ref, *rest):
    tokens, columns = 128, own_ref.shape[1]
    total = own_ref[...] + got_ref[...].astype(f32)
    if counted:
        out_ref, later_ref = rest
        counts = total[tokens : tokens + 1, :128]
        inverse = jnp.where(counts > 0.0, 1.0 / (DOCS * jnp.maximum(counts, 1.0)), 0.0)
        lane = lax.broadcasted_iota(jnp.int32, (tokens, 128), 1)
        here = lane == lax.broadcasted_iota(jnp.int32, (tokens, 128), 0)
        weights = []
        for step in range(2):
            ids = jnp.where(here, total[tokens + 1 + step : tokens + 2 + step, :128], 0.0)
            ids = jnp.sum(ids, axis=-1, keepdims=True).astype(jnp.int32) + DOCS * step
            hot = jnp.where(lane == ids, inverse, 0.0)
            weights.append(jnp.sum(hot, axis=-1, keepdims=True))
        weight = weights[0]
        later_ref[...] = jnp.broadcast_to(weights[1], later_ref.shape)
    else:
        weight_ref, out_ref = rest
        weight = weight_ref[:, :1]
    error = total[:tokens] * scale
    grad = (weight * error / columns).astype(bf16)
    each = jnp.sum(error * error, axis=-1, keepdims=True) / columns
    loss = jnp.sum(weight * 0.5 * each, axis=0, keepdims=True)
    high = loss.astype(bf16).astype(f32)
    middle = (loss - high).astype(bf16).astype(f32)
    low = loss - high - middle
    lane = lax.broadcasted_iota(jnp.int32, (EXTRA, columns), 1)
    lane = lane + columns * lax.broadcasted_iota(jnp.int32, (EXTRA, columns), 0)
    row = jnp.where(lane == 0, high, jnp.where(lane == 1, middle, jnp.where(lane == 2, low, 0.0)))
    row = row.astype(bf16)
    for at in range(out_ref.shape[0]):
        out_ref[at, :tokens] = grad
        out_ref[at, tokens:] = row


def errors(own, got, weight, tokens, copies, scale):
    columns = own.shape[1]
    sent = jax.ShapeDtypeStruct((copies, tokens + EXTRA, columns), bf16)
    kept = jax.ShapeDtypeStruct((tokens, 128), f32)
    counted = weight is None
    return pl.pallas_call(
        functools.partial(error_kernel, scale, counted),
        out_shape=(sent, kept) if counted else sent,
        compiler_params=pltpu.CompilerParams(vmem_limit_bytes=VMEM),
        cost_estimate=pl.CostEstimate(
            flops=8 * tokens * columns, bytes_accessed=30 * tokens * columns, transcendentals=0
        ),
        name="errors",
    )(own, got, *(() if counted else (weight,)))


def project_kernel(columns_ref, weights_ref, counts_ref, out_ref, first_ref, later_ref, made, sent):
    shards, _, rows, _ = columns_ref.shape
    groups, block, _ = made.shape
    tokens = block - EXTRA
    share = tokens // rows

    def give(at):
        return pltpu.make_async_copy(made.at[pl.ds(at, 2)], out_ref.at[pl.ds(at, 2)], sent.at[at // 2])

    for at in range(0, groups, 2):
        for shard in range(at * share, (at + 2) * share):
            row = shard * rows + shard // share * EXTRA
            first_ref[row : row + rows] = columns_ref[shard, 0]
        for group in (at, at + 1):
            row = group * block + tokens
            first_ref[row : row + EXTRA] = jnp.zeros((EXTRA, first_ref.shape[1]), bf16)
        product = jnp.dot(
            first_ref[at * block : (at + 2) * block], weights_ref[0], preferred_element_type=f32
        ).astype(bf16)
        for group in range(2):
            made[at + group, :tokens] = product[group * block : group * block + tokens]
            made[at + group, tokens:] = counts_ref[...]
        give(at).start()
    for shard in range(shards):
        later_ref[shard * rows : (shard + 1) * rows] = columns_ref[shard, 1]
    for at in range(0, groups, 2):
        give(at).wait()


def project(columns, weights, count_rows, groups):
    shards, _, rows, features = columns.shape
    tokens, wide = shards * rows, weights.shape[2]
    block = jax.ShapeDtypeStruct((groups, tokens // groups + EXTRA, wide), bf16)
    plain = jax.ShapeDtypeStruct((tokens, features), bf16)
    spaced = jax.ShapeDtypeStruct((tokens + groups * EXTRA, features), bf16)
    vmem = pl.BlockSpec(memory_space=pltpu.MemorySpace.VMEM)
    return pl.pallas_call(
        project_kernel,
        in_specs=[vmem, vmem, vmem],
        out_specs=(pl.BlockSpec(memory_space=pl.ANY), vmem, vmem),
        out_shape=(block, spaced, plain),
        scratch_shapes=[pltpu.VMEM(block.shape, bf16), pltpu.SemaphoreType.DMA((groups // 2,))],
        compiler_params=pltpu.CompilerParams(vmem_limit_bytes=VMEM),
        name="project",
    )(columns, weights, count_rows)


def body(hidden, targets, doc_ids, weights, adam_m, adam_v, anchor, momentum, fragment):
    steps_total, rows, model_width = hidden.shape[1:]
    shard_rows, value_width = weights.shape[1:]
    frag_width = anchor.shape[1]
    nx, nn, nf = (lax.axis_size(a) for a in ORDER)
    shards, groups = nx * nn * nf, nx * nn
    f_at, c_at = lax.axis_index("zf"), lax.axis_index("c")
    scale = model_width ** (-0.5)
    zero = jnp.zeros((), jnp.int32)
    start = fragment[0] * frag_width
    replicas = lax.axis_size(REPLICA)
    tokens = nf * rows

    def pick(array, at, axis):
        return lax.dynamic_index_in_dim(array, at, axis, keepdims=False)

    blocks = normalize(hidden, shards)
    blocks, weights, targets, doc_ids = tie(blocks, weights, targets, doc_ids)
    columns = exchange(blocks, ORDER)

    doc_range = jnp.arange(DOCS, dtype=jnp.int32)
    counts = jnp.sum((doc_ids[0][..., None] == doc_range).astype(f32), axis=1)
    count_rows = jnp.pad(
        counts.reshape(1, -1).astype(bf16),
        ((0, EXTRA - 1), (0, value_width - steps_total * DOCS)),
    )
    goal = targets[0].astype(f32) / scale
    goal = jnp.concatenate([jnp.where(f_at == at, goal, 0.0) for at in range(nf)], axis=1)
    ids = doc_ids[0].astype(f32)
    ids = jnp.concatenate([jnp.where(f_at == at, ids, 0.0) for at in range(nf)], axis=1)
    ids = jnp.pad(ids, ((1, EXTRA - 1 - steps_total), (0, value_width - tokens)))
    goal = [jnp.concatenate([goal[0], -ids], axis=0), goal[1]]

    half = shard_rows // 2
    local = lax.dynamic_slice(weights[0], (zero, start), (shard_rows, frag_width))
    local = local.reshape(2, half, frag_width)
    summed = pick(local, c_at, 0).astype(f32) + swap(pick(local, c_at ^ 1, 0), "c").astype(f32)
    y_at = lax.rem(lax.axis_index("y"), 2)
    summed = summed.reshape(2, half // 2, frag_width)
    summed = pick(summed, y_at, 0) + swap(pick(summed, y_at ^ 1, 0), "y")
    for axis, bit in (("y", 2), ("y", 4), ("zh", 1)):
        summed = summed + swap(summed, axis, bit)

    def whole(mine, other, at):
        return jnp.concatenate([jnp.where(at == 0, mine, other), jnp.where(at == 0, other, mine)])

    columns, goal, count_rows, summed = tie(columns, goal, count_rows, summed)
    partial, *step_rows = project(columns, weights, count_rows, groups)

    master = weights[0].astype(f32)
    first = adam_m[0].astype(f32)
    second = adam_v[0].astype(f32)
    anchor_rows = anchor.astype(f32)
    loss_rows, weight = [], None
    for step in range(steps_total):
        rows_now = step_rows[step]
        if step == 1:
            partial = jnp.dot(rows_now, master.astype(bf16), preferred_element_type=f32)
            partial = partial.astype(bf16).reshape(groups, tokens, value_width)
            partial, summed = tie(partial, summed)
        partial = exchange(partial, GROUP)
        if step == 1:
            summed = whole(summed, swap(summed, "y"), y_at)
            partial, summed = tie(partial, summed)
        own = jnp.sum(partial.astype(f32), axis=0) - goal[step]
        got = swap(own.astype(bf16), "zf")
        sent = errors(own, got, weight, tokens, groups, scale)
        if step == 0:
            sent, weight = sent
        sent, summed = tie(sent, summed)
        got = exchange(sent, GROUP)
        if step == 0:
            got, summed = tie(got, summed)
        else:
            summed = whole(summed, swap(summed, "c"), c_at)
            mean_delta = anchor_rows - summed / replicas
            new_moment = NESTEROV * momentum.astype(f32) + mean_delta
            global_fragment = anchor_rows - OUTER_RATE * (mean_delta + NESTEROV * new_moment)
            got, global_fragment = tie(got, global_fragment)
        loss_rows.append(got[:, tokens, :128])
        everyone = (got if step == 0 else got[:, :tokens]).reshape(-1, value_width)
        gradient = (
            lax.dot_general(
                rows_now, everyone, (((0,), (0,)), ((), ())), preferred_element_type=f32
            )
            * scale
        )
        master, first, second = adam_update(master, first, second, gradient)

    merged = (
        MIXING * lax.dynamic_slice(master, (zero, start), (shard_rows, frag_width))
        + (1.0 - MIXING) * global_fragment
    )
    master = lax.dynamic_update_slice(master, merged, (zero, start))
    losses = jnp.sum(jnp.stack(loss_rows).astype(f32), axis=(1, 2))
    return (master[None], losses[None])


def solution(mesh):
    fine = Mesh(mesh.devices.reshape(2, 8, 2, 4, 2, 2), REPLICA + FSDP)
    placed = (
        P(REPLICA, None, FSDP, None),
        P(REPLICA, None, FSDP, None),
        P(REPLICA, None, FSDP),
        P(REPLICA, FSDP, None),
        P(REPLICA, FSDP, None),
        P(REPLICA, FSDP, None),
        P(FSDP, None),
        P(FSDP, None),
        P(),
    )
    return jax.shard_map(
        body,
        mesh=fine,
        in_specs=placed,
        out_specs=(P(REPLICA, FSDP, None), P(REPLICA, None)),
        check_vma=False,
    )
```
